32 devices in a mesh: grp: 2 (over y), pb: 4 (over z), ea: 2 (over x), ma: 2 (over core).
Axes of the slice: x: 2, y: 2, z: 4, core: 2. Of those that a mesh axis runs over, the one named last changes fastest.
Arguments:
- table: bfloat16 [2, 4, 4, 60, 1024], P(None, 'pb', 'ea', 'ma'), may hold values from -1.5 to 1.5
- r_el: int32 [4, 3], P('ea'), may hold values from -6 to 6
- r_ph: int32 [4, 3], replicated, may hold values from -6 to 6
- k_coords: int32 [8, 3], P('grp'), parts along dimension 0, may hold values from 0 to 47
- q_coords: int32 [192, 3], P(('grp', 'pb')), parts along dimension 0, may hold values from 0 to 47
- u_k: bfloat16 [2, 8, 32, 32], P(None, ('grp', 'ea')), parts along dimension 1, may hold values from -0.75 to 0.75
- u_kq: bfloat16 [2, 192, 4, 32, 32], P(None, ('grp', 'pb', 'ma'), 'ea'), parts along dimension 1, may hold values from -0.75 to 0.75
- modes_q: bfloat16 [2, 192, 60, 60], P(None, ('grp', 'pb', 'ma')), parts along dimension 1, may hold values from -0.5 to 0.5
- weights_q: float32 [192, 60], P(('grp', 'pb', 'ma')), parts along dimension 0, may hold values from 0.2 to 6
Outputs:
- coupling_sq: bfloat16 [192, 4, 60, 1024], P(('grp', 'pb', 'ma'), 'ea'), parts along dimension 0
- kernel: float32 [8, 1024], P(('grp', 'ea')), parts along dimension 0
The draws below stay inside these ranges and needn't reach their ends.
There are 2 independent parts, one for each index of `grp`. The reference program is written for one: setup_inputs(seed, part) draws one part's arguments, and reference() takes and returns one part's arrays. A program takes and returns all parts, laid end to end along the dimension named above; an argument that names none is the same for every part. Nothing has to cross between parts.
All inputs are finite; a program needn't handle non-finite values.
Results may differ from the reference program's by a relative error of at most 0.0084.
Values may be sent and summed in bfloat16 or wider, within the bound.
No kernel may reach another device: no remote copies, remote signals or barrier semaphores. Data moves between devices by JAX's collectives and lax.ppermute only.
A program may use at most 128 MiB of HBM per device.

```python
import math
import jax
import jax.numpy as jnp
from jax import lax

W = 32
MODES = 60
GRID = 48
Q_DEV = 12
NRE = 4
NRP = 4
NK = 4
NQ = 96
N_PB = 4
N_MA = 2


def draw_weights_q(key, part):
    key = jax.random.fold_in(key, 7)
    ramp = 3.0 ** (jnp.arange(NQ, dtype=jnp.float32) / (NQ - 1))
    base = jnp.exp(jax.random.uniform(key, (NQ, MODES), jnp.float32, math.log(0.2), math.log(2.0)))
    return base * ramp[:, None]


def with_ends(drawn, stream_key, low, largest):
    longest = drawn.shape.index(max(drawn.shape))
    spots = []
    for shift in (0, 1):
        where = [jax.random.randint(jax.random.fold_in(stream_key, axis), (), 0, length) for axis, length in enumerate(drawn.shape)]
        where[longest] = (where[longest] + shift) % drawn.shape[longest]
        spots.append(tuple(where))
    return drawn.at[spots[0]].set(low).at[spots[1]].set(largest)


def steps_of(rng, dims, shards, low, largest):
    loudness, own = 1.0, jax.random.fold_in(rng, 6)
    for axis_at, shards_of in shards:
        heights = jnp.exp(jax.random.uniform(jax.random.fold_in(own, axis_at), (shards_of,), jnp.float32, low / len(shards), largest / len(shards)))
        loudness = loudness * jnp.repeat(heights, dims[axis_at] // shards_of).reshape([-1 if axis == axis_at else 1 for axis in range(len(dims))])
    return loudness


def bell_draw(own_key, extent, scale, most, pieces=(), kind=jnp.bfloat16):
    drawn = jax.random.normal(own_key, extent, jnp.float32) * scale
    if len(pieces) > 0:
        drawn = steps_of(own_key, extent, pieces, -0.22, 0.18) * drawn
    return jnp.clip(drawn, min=-most, max=most).astype(kind)


def setup_inputs(seed: int = 0, part: int = 0) -> dict:
    key_of = jax.random.split(jax.random.key(seed), 10)
    part_splits = jax.random.split(jax.random.fold_in(key_of[9], part), 10)
    return {
        "table": bell_draw(key_of[0], (2, NRP, NRE, MODES, W * W), (NRE * NRP) ** -0.5, 1.5, ((1, 4), (2, 2), (3, 2))),
        "r_el": with_ends(jax.random.randint(key_of[1], (NRE, 3), -6, 7), jax.random.fold_in(key_of[1], 1), -6, 6).astype(jnp.int32),
        "r_ph": with_ends(jax.random.randint(key_of[2], (NRP, 3), -6, 7), jax.random.fold_in(key_of[2], 1), -6, 6).astype(jnp.int32),
        "k_coords": with_ends(jax.random.randint(part_splits[3], (NK, 3), 0, GRID), jax.random.fold_in(part_splits[3], 1), 0, GRID - 1).astype(jnp.int32),
        "q_coords": with_ends(jax.random.randint(part_splits[4], (NQ, 3), 0, GRID), jax.random.fold_in(part_splits[4], 1), 0, GRID - 1).astype(jnp.int32),
        "u_k": bell_draw(part_splits[5], (2, NK, W, W), (2 * W) ** -0.5, 0.75, ((1, 2),)),
        "u_kq": bell_draw(part_splits[6], (2, NQ, NK, W, W), (2 * W) ** -0.5, 0.75, ((1, 8), (2, 2))),
        "modes_q": bell_draw(part_splits[7], (2, NQ, MODES, MODES), (2 * MODES) ** -0.5, 0.5, ((1, 8),)),
        "weights_q": draw_weights_q(jax.random.fold_in(jax.random.fold_in(key_of[9], part), 71), part),
    }


def phase_pair(coords, vectors):
    turns = jnp.mod(jnp.sum(coords[:, None, :] * vectors[None, :, :], axis=-1), GRID)
    angles = turns.astype(jnp.float32) * (2.0 * math.pi / GRID)
    return jnp.cos(angles), jnp.sin(angles)


def rotation_block(cos_part, sin_part):
    return jnp.stack([jnp.stack([cos_part, -sin_part], 1), jnp.stack([sin_part, cos_part], 1)], 0)


def rounded(values):
    return lax.optimization_barrier(values.astype(jnp.bfloat16)).astype(jnp.float32)


def reference(table, r_el, r_ph, k_coords, q_coords, u_k, u_kq, modes_q, weights_q):
    electron = rounded(rotation_block(*phase_pair(k_coords, r_el)))
    by_k = rounded(jnp.einsum('dkce,cpemx->kdpmx', electron, table.astype(jnp.float32)))
    right_block = jnp.stack([jnp.stack([u_k[0], u_k[1]], 2), jnp.stack([-u_k[1], u_k[0]], 2)], 0).astype(jnp.float32)
    group = Q_DEV * N_MA
    coords_all = q_coords.reshape(N_PB, group, 3)
    pairs_all = jnp.swapaxes(u_kq.reshape(2, N_PB, group, NK, W, W), 0, 1)
    modes_all = jnp.swapaxes(modes_q.reshape(2, N_PB, group, MODES, MODES), 0, 1)
    weights_all = weights_q.reshape(N_PB, group, MODES)

    def one_group(inputs):
        coords, pair_rot, mode_rot, weight_rows = inputs
        phonon = rounded(rotation_block(*phase_pair(coords, r_ph)))
        summed = rounded(jnp.einsum('dqcp,kcpmx->dqkmx', phonon, by_k))
        shaped = summed.reshape(2, group, NK, MODES, W, W)
        right = rounded(jnp.einsum('cqkamn,cknds->dqkams', shaped, right_block))
        flipped = jnp.swapaxes(pair_rot, -1, -2)
        left_block = jnp.stack([jnp.stack([flipped[0], flipped[1]], 3), jnp.stack([-flipped[1], flipped[0]], 3)], 0).astype(jnp.float32)
        band = rounded(jnp.einsum('dqkrcm,cqkams->dqkars', left_block, right)).reshape(2, group, NK, MODES, W * W)
        mode_block = jnp.stack([jnp.stack([mode_rot[0], mode_rot[1]], 2), jnp.stack([-mode_rot[1], mode_rot[0]], 2)], 0).astype(jnp.float32)
        coupling = jnp.einsum('cqkax,cqadv->dqkvx', band, mode_block)
        squared = coupling[0] * coupling[0] + coupling[1] * coupling[1]
        weighted = jnp.sum(weight_rows[:, None, :, None] * squared, axis=(0, 2))
        return squared.astype(jnp.bfloat16), weighted

    squared_all, weighted_all = lax.map(one_group, (coords_all, pairs_all, modes_all, weights_all))
    coupling_sq = squared_all.reshape(NQ, NK, MODES, W * W)
    kernel = jnp.sum(weighted_all, axis=0) / (NQ * MODES)
    return coupling_sq, kernel
```

```python
import functools
import math

import jax
import jax.numpy as jnp
from jax import lax
from jax.experimental import pallas as pl
from jax.experimental.pallas import tpu as pltpu
from jax.sharding import PartitionSpec as P

GRID = 48
MIB = 1 << 20
NT = (((1,), (1,)), ((), ()))
F32 = jnp.float32
BF16 = jnp.bfloat16
MODE_PAD = 32
BRANCH_PAD = 64
SMEM = pl.BlockSpec(memory_space=pltpu.SMEM)
VMEM = pl.BlockSpec(memory_space=pltpu.VMEM)


def wrap(turns):
    turns = lax.rem(turns, GRID)
    return jnp.where(turns < 0, turns + GRID, turns)


def phases(turns):
    angles = turns.astype(F32) * (2.0 * math.pi / GRID)
    return jnp.cos(angles).astype(BF16).astype(F32), jnp.sin(angles).astype(BF16).astype(F32)


def electron_kernel(n_k, n_src, rows_e, half, place_ref, k_ref, *refs):
    vectors, tables, outs = refs[:n_src], refs[n_src : 2 * n_src], refs[2 * n_src :]
    turns = []
    for k in range(n_k):
        for s in range(n_src):
            for e in range(rows_e):
                row = place_ref[0] * n_k + k
                t = sum(k_ref[row, d] * vectors[s][e, d] for d in range(3))
                turns.append(jnp.full((1, 128), wrap(t), jnp.int32))
    cos, sin = phases(jnp.concatenate(turns, 0))
    wide = half * rows_e
    at = lax.broadcasted_iota(jnp.int32, (MODE_PAD, 2 * wide), 0)
    lane = lax.broadcasted_iota(jnp.int32, (MODE_PAD, 2 * wide), 1)
    imag = lane >= wide
    rest = jnp.where(imag, lane - wide, lane)
    own = rest - at * rows_e
    rows = []
    for k in range(n_k):
        for out in range(2):
            columns = []
            for s in range(n_src):
                value = jnp.zeros((MODE_PAD, 2 * wide), F32)
                for e in range(rows_e):
                    i = (k * n_src + s) * rows_e + e
                    c, d = cos[i : i + 1, : 2 * wide], sin[i : i + 1, : 2 * wide]
                    here = jnp.where(imag, c, d) if out else jnp.where(imag, -d, c)
                    value = jnp.where(own == e, here, value)
                columns.append(value)
            rows.append(jnp.concatenate(columns, 1))
    factor = jnp.concatenate(rows, 0).astype(BF16)
    data = jnp.concatenate(
        [t[c, 0].reshape(wide, t.shape[-1]) for t in tables for c in range(2)], 0
    )
    total = jnp.dot(factor, data, preferred_element_type=F32).astype(BF16)
    for k in range(n_k):
        outs[k][...] = total[k * 2 * MODE_PAD : (k + 1) * 2 * MODE_PAD]


def rotation_kernel(masks, place_ref, r_ref, q_ref, u_k_ref, u_kq_ref, left_ref, kron_ref):
    _, q_rows, n_k, width, _ = u_kq_ref.shape
    lanes = lax.broadcasted_iota(jnp.int32, (1, q_rows * width), 1) // width
    first = place_ref[2] * q_rows
    coords = []
    for d in range(3):
        line = jnp.zeros((1, q_rows * width), jnp.int32)
        for q in range(q_rows):
            line = jnp.where(lanes == q, q_ref[first + q, d], line)
        coords.append(line)
    turns = []
    for mask in masks:
        p = place_ref[1] ^ mask
        turns.append(wrap(sum(coords[d] * r_ref[p, d] for d in range(3))))
    cos, sin = phases(jnp.concatenate(turns, 0))
    row = lax.broadcasted_iota(jnp.int32, (8 * width, 8 * width), 0)
    lane = lax.broadcasted_iota(jnp.int32, (8 * width, 8 * width), 1)
    same = row % 8 == lane // width
    for k in range(n_k):
        ur, ui = (
            jnp.concatenate([u_kq_ref[c, q, k].astype(F32) for q in range(q_rows)], 1)
            for c in range(2)
        )
        parts = []
        for i in range(len(masks)):
            c, s = cos[i : i + 1], sin[i : i + 1]
            parts += [c * ur + s * ui, s * ur - c * ui]
        left_ref[k] = jnp.concatenate(parts, 0).T.astype(BF16)
        for c in range(2):
            u = u_k_ref[c, k].astype(F32).T
            u = jnp.concatenate([u] * 8, 1)
            u = jnp.broadcast_to(u[:, None, :], (width, 8, 8 * width)).reshape(8 * width, 8 * width)
            kron_ref[k, :, c * 8 * width : (c + 1) * 8 * width] = jnp.where(same, u, 0.0).astype(BF16)


def mode_kernel(half, place_ref, modes_ref, weights_ref, mix_ref, column_ref):
    _, q_rows, modes, _ = modes_ref.shape
    first = place_ref[2] == 0
    rows = jnp.zeros((MODE_PAD - half, 2 * BRANCH_PAD), F32)
    gap = jnp.zeros((half, BRANCH_PAD - modes), F32)
    for q in range(q_rows):
        dr, di = modes_ref[0, q].astype(F32), modes_ref[1, q].astype(F32)
        parts = []
        for h in range(2):
            r, i = (jnp.where(first ^ (h == 1), d[:half], d[half:]) for d in (dr, di))
            parts += [jnp.concatenate([r, gap, i, gap], 1), rows]
            parts += [jnp.concatenate([-i, gap, r, gap], 1), rows]
        mix_ref[q] = jnp.concatenate(parts, 0).T.astype(BF16)
    w = weights_ref[...]
    w = jnp.concatenate([w, jnp.zeros((q_rows, 128 - modes), F32)], 1)
    w = jnp.concatenate([w, jnp.zeros((128 - q_rows, 128), F32)], 0).T
    for q in range(q_rows):
        column_ref[q] = w[:BRANCH_PAD, q : q + 1]


def coupling_kernel(n_p, k, width, q_step, modes, count, *refs):
    own, sib = refs[:n_p], refs[n_p : 2 * n_p]
    a_ref, l_ref, d_ref, w_ref = refs[2 * n_p : 2 * n_p + 4]
    out_ref, mean_ref, x2, zs, acc = refs[-5:]
    step = pl.program_id(0)
    q_all = l_ref.shape[1] // width
    pitch = width + 8
    unroll = 4

    @pl.when(step == 0)
    def _():
        acc[...] = jnp.zeros_like(acc)
        a_mat = a_ref[0]
        for p in range(n_p):
            for t in range(width // 16):
                parts = []
                for u in range(2):
                    lanes = pl.ds((2 * t + u) * 8 * width, 8 * width)
                    ys = []
                    for ref in (own[p], sib[p]):
                        y = ref[:, lanes]
                        h = y.shape[0] // 2
                        ys.append((y, jnp.concatenate([-y[h:], y[:h]], 0)))
                    y0 = jnp.concatenate([ys[0][0], ys[1][0]], 0)
                    y1 = jnp.concatenate([ys[0][1], ys[1][1]], 0)
                    rhs = jnp.concatenate(
                        [jnp.concatenate([y0, y1], 1), jnp.concatenate([y1, -y0], 1)], 0
                    )
                    parts.append(lax.dot_general(a_mat, rhs, NT, preferred_element_type=F32))
                for n in range(width):
                    both = jnp.concatenate([part[n * 8 : n * 8 + 8] for part in parts], 0).astype(BF16)
                    for c in range(2):
                        row = (p * 2 + c) * width + t * 16
                        x2[row : row + 16, n * 128 : (n + 1) * 128] = both[:, c * 128 : (c + 1) * 128]

        def columns(i, carry):
            start = pl.multiple_of(i * unroll * 128, unroll * 128)
            z = jnp.dot(l_ref[0], x2[:, pl.ds(start, unroll * 128)], preferred_element_type=F32)
            for u in range(unroll):
                zs[pl.ds(unroll * i + u, q_all * width, stride=pitch), :] = z[:, u * 128 : (u + 1) * 128]
            return carry

        lax.fori_loop(0, width // unroll, columns, 0)

    rows = width * pitch
    total = acc[...]
    for u in range(q_step):
        q = step * q_step + u
        z = zs[pl.ds(pl.multiple_of(q * rows, rows), rows), :]
        z = z.reshape(width, pitch, 128)[:, :width].reshape(width * width, 128).astype(BF16)
        res = lax.dot_general(d_ref[u], z, NT, preferred_element_type=F32)
        sq = res[:BRANCH_PAD] * res[:BRANCH_PAD] + res[BRANCH_PAD:] * res[BRANCH_PAD:]
        out_ref[u, 0] = sq[:modes].astype(BF16)
        weighted = sq * w_ref[u]
        for r in range(BRANCH_PAD // 8):
            total = total + weighted[r * 8 : r * 8 + 8]
    acc[...] = total

    @pl.when(step == pl.num_programs(0) - 1)
    def _():
        mean = jnp.sum(total, 0, keepdims=True) / count
        if k == 0:
            mean_ref[...] = jnp.broadcast_to(mean, mean_ref.shape)
        else:
            mean_ref[...] = refs[2 * n_p + 4][...]
            mean_ref[k : k + 1] = mean


def body(table, r_el, r_ph, k_coords, q_coords, u_k, u_kq, modes_q, weights_q):
    n_ea, n_pb, n_ma = lax.axis_size("ea"), lax.axis_size("pb"), lax.axis_size("ma")
    ea, pb, ma = lax.axis_index("ea"), lax.axis_index("pb"), lax.axis_index("ma")
    k_rows, q_rows, width = u_k.shape[1], u_kq.shape[1], u_k.shape[2]
    rows_e, half, pairs = table.shape[2], table.shape[3], table.shape[4]
    modes = n_ma * half
    place = jnp.stack([ea, pb, ma]).astype(jnp.int32)
    shift = lambda n, s: [(i, (i + s) % n) for i in range(n)]
    flip = lambda n, s: [(i, i ^ s) for i in range(n)]

    table = jnp.transpose(table, (0, 1, 3, 2, 4))
    tables = [table] + [lax.ppermute(table, "ea", shift(n_ea, s)) for s in range(1, n_ea)]
    vectors = [r_el] + [lax.ppermute(r_el, "ea", shift(n_ea, s)) for s in range(1, n_ea)]

    masks = [0]
    distance = n_pb // 2
    while distance:
        masks += [m ^ distance for m in masks]
        distance //= 2

    left, kron = pl.pallas_call(
        functools.partial(rotation_kernel, masks),
        out_shape=[
            jax.ShapeDtypeStruct((k_rows, q_rows * width, n_pb * 2 * width), BF16),
            jax.ShapeDtypeStruct((k_rows, 8 * width, 16 * width), BF16),
        ],
        in_specs=[SMEM, SMEM, SMEM, VMEM, VMEM],
        out_specs=[VMEM, VMEM],
        cost_estimate=pl.CostEstimate(flops=1 << 20, bytes_accessed=4 * MIB, transcendentals=0),
        compiler_params=pltpu.CompilerParams(vmem_limit_bytes=24 * MIB),
        name="rotations",
    )(place, r_ph, q_coords, u_k, u_kq)

    by_k = pl.pallas_call(
        functools.partial(electron_kernel, k_rows, n_ea, rows_e, half),
        out_shape=[jax.ShapeDtypeStruct((2 * MODE_PAD, pairs), BF16)] * k_rows,
        in_specs=[SMEM] * (2 + n_ea) + [VMEM] * n_ea,
        out_specs=[VMEM] * k_rows,
        compiler_params=pltpu.CompilerParams(vmem_limit_bytes=16 * MIB),
        name="electron_sum",
    )(place, k_coords, *vectors, *tables)

    mix, weights = pl.pallas_call(
        functools.partial(mode_kernel, half),
        out_shape=[
            jax.ShapeDtypeStruct((q_rows, 2 * BRANCH_PAD, n_ma * 2 * MODE_PAD), BF16),
            jax.ShapeDtypeStruct((q_rows, BRANCH_PAD, 1), F32),
        ],
        in_specs=[SMEM, VMEM, VMEM],
        out_specs=[VMEM, VMEM],
        cost_estimate=pl.CostEstimate(flops=1 << 20, bytes_accessed=4 * MIB, transcendentals=0),
        compiler_params=pltpu.CompilerParams(vmem_limit_bytes=16 * MIB),
        name="mode_rotation",
    )(place, modes_q, weights_q)

    swap = flip(n_ma, 1)
    blocks = [[y] for y in by_k]
    distance = n_pb // 2
    while distance:
        for held in blocks:
            held += [lax.ppermute(y, "pb", flip(n_pb, distance)) for y in held]
        distance //= 2

    q_step = q_rows // 2 if q_rows % 2 == 0 else q_rows
    out = mean = None
    for k in range(k_rows):
        own = blocks[k]
        sib = [lax.ppermute(y, "ma", swap) for y in own]
        operands = [*own, *sib, kron, left, mix, weights]
        in_specs = (
            [VMEM] * (2 * n_pb)
            + [
                pl.BlockSpec((1, 8 * width, 16 * width), functools.partial(lambda k, i: (k, 0, 0), k)),
                pl.BlockSpec(
                    (1, q_rows * width, n_pb * 2 * width), functools.partial(lambda k, i: (k, 0, 0), k)
                ),
                pl.BlockSpec((q_step, 2 * BRANCH_PAD, n_ma * 2 * MODE_PAD), lambda i: (i, 0, 0)),
                pl.BlockSpec((q_step, BRANCH_PAD, 1), lambda i: (i, 0, 0)),
            ]
        )
        aliases = {}
        if k:
            in_specs += [VMEM, pl.BlockSpec(memory_space=pl.ANY)]
            aliases = {len(operands) + 1: 0}
            operands += [mean, out]
        out, mean = pl.pallas_call(
            functools.partial(
                coupling_kernel, n_pb, k, width, q_step, modes, q_rows * n_pb * n_ma * modes
            ),
            grid=(q_rows // q_step,),
            out_shape=[
                jax.ShapeDtypeStruct((q_rows, k_rows, modes, pairs), BF16),
                jax.ShapeDtypeStruct((k_rows, pairs), F32),
            ],
            in_specs=in_specs,
            out_specs=[
                pl.BlockSpec((q_step, 1, modes, pairs), functools.partial(lambda k, i: (i, k, 0, 0), k)),
                pl.BlockSpec((k_rows, pairs), lambda i: (0, 0)),
            ],
            scratch_shapes=[
                pltpu.VMEM((n_pb * 2 * width, width * 128), BF16),
                pltpu.VMEM((q_rows * width * (width + 8), 128), F32),
                pltpu.VMEM((8, pairs), F32),
            ],
            input_output_aliases=aliases,
            compiler_params=pltpu.CompilerParams(vmem_limit_bytes=(16 + 2 * n_pb) * MIB),
            name="coupling",
        )(*operands)
    mean = mean + lax.ppermute(mean, "ma", swap)
    distance = 1
    while distance < n_pb:
        mean = mean + lax.ppermute(mean, "pb", flip(n_pb, distance))
        distance *= 2
    return (out, mean)


def solution(mesh):
    return jax.shard_map(
        body,
        mesh=mesh,
        in_specs=(
            P(None, "pb", "ea", "ma", None),
            P("ea", None),
            P(),
            P("grp", None),
            P(("grp", "pb"), None),
            P(None, ("grp", "ea"), None, None),
            P(None, ("grp", "pb", "ma"), "ea", None, None),
            P(None, ("grp", "pb", "ma"), None, None),
            P(("grp", "pb", "ma"), None),
        ),
        out_specs=(P(("grp", "pb", "ma"), "ea", None, None), P(("grp", "ea"), None)),
        check_vma=False,
    )
```

```python
import functools
import math

import jax
import jax.numpy as jnp
from jax import lax
from jax.experimental import pallas as pl
from jax.experimental.pallas import tpu as pltpu
from jax.sharding import PartitionSpec as P

GRID = 48
MIB = 1 << 20
NT = (((1,), (1,)), ((), ()))
F32 = jnp.float32
BF16 = jnp.bfloat16
MODE_PAD = 32
BRANCH_PAD = 64
SMEM = pl.BlockSpec(memory_space=pltpu.SMEM)
VMEM = pl.BlockSpec(memory_space=pltpu.VMEM)
HBM = pl.BlockSpec(memory_space=pltpu.HBM)


def cost(us):
    return pl.CostEstimate(flops=us * 1_000_000_000, bytes_accessed=us * 3_000_000, transcendentals=0)


def wrap(turns):
    turns = lax.rem(turns, GRID)
    return jnp.where(turns < 0, turns + GRID, turns)


def phases(turns):
    angles = turns.astype(F32) * (2.0 * math.pi / GRID)
    return jnp.cos(angles).astype(BF16).astype(F32), jnp.sin(angles).astype(BF16).astype(F32)


def phase_kernel(n_k, n_ea, rows_e, half, coords_ref, factor_ref):
    here, core = lax.axis_index("ea"), lax.axis_index("ma")
    turns = []
    for s in range(n_ea):
        for i in range(n_k):
            row = lax.rem(here + s, n_ea) * n_k + lax.rem(core + i, n_k)
            for e in range(rows_e):
                t = sum(coords_ref[row, d] * coords_ref[n_ea * n_k + e, d] for d in range(3))
                turns.append(jnp.full((1, 128), wrap(t), jnp.int32))
    cos, sin = phases(jnp.concatenate(turns, 0))
    wide = half * rows_e
    at = lax.broadcasted_iota(jnp.int32, (MODE_PAD, 2 * wide), 0)
    lane = lax.broadcasted_iota(jnp.int32, (MODE_PAD, 2 * wide), 1)
    imag = lane >= wide
    own = jnp.where(imag, lane - wide, lane) - at * rows_e
    rows = []
    for i in range(n_ea * n_k):
        for out in range(2):
            value = jnp.zeros((MODE_PAD, 2 * wide), F32)
            for e in range(rows_e):
                j = i * rows_e + e
                c, d = cos[j : j + 1, : 2 * wide], sin[j : j + 1, : 2 * wide]
                value = jnp.where(own == e, jnp.where(imag, c, d) if out else jnp.where(imag, -d, c), value)
            rows.append(value)
    factor_ref[...] = jnp.concatenate(rows, 0).astype(BF16)


def electron_kernel(factor_ref, table_ref, *outs):
    _, _, half, rows_e, pairs = table_ref.shape
    data = jnp.concatenate([table_ref[c, 0].reshape(half * rows_e, pairs) for c in range(2)], 0)
    total = jnp.dot(factor_ref[...], data, preferred_element_type=F32)
    for i, out in enumerate(outs):
        out[...] = total[i * 2 * MODE_PAD : (i + 1) * 2 * MODE_PAD].astype(out.dtype)


def rotation_kernel(masks, r_ref, q_ref, u_k_ref, u_kq_ref, left_ref, kron_ref):
    _, q_rows, n_k, width, _ = u_kq_ref.shape
    lanes = lax.broadcasted_iota(jnp.int32, (1, q_rows * width), 1) // width
    first = lax.axis_index("ma") * q_rows
    coords = []
    for d in range(3):
        line = jnp.zeros((1, q_rows * width), jnp.int32)
        for q in range(q_rows):
            line = jnp.where(lanes == q, q_ref[d, first + q], line)
        coords.append(line)
    turns = []
    for mask in masks:
        p = lax.axis_index("pb") ^ mask
        turns.append(wrap(sum(coords[d] * r_ref[p, d] for d in range(3))))
    cos, sin = phases(jnp.concatenate(turns, 0))
    row = lax.broadcasted_iota(jnp.int32, (8 * width, 8 * width), 0)
    lane = lax.broadcasted_iota(jnp.int32, (8 * width, 8 * width), 1)
    same = row % 8 == lane // width
    for k in range(n_k):
        at = lax.rem(lax.axis_index("ma") + k, n_k)
        ur, ui = (
            jnp.concatenate([u_kq_ref[c, q, at].astype(F32) for q in range(q_rows)], 1)
            for c in range(2)
        )
        parts = []
        for i in range(len(masks)):
            c, s = cos[i : i + 1], sin[i : i + 1]
            parts += [c * ur + s * ui, s * ur - c * ui]
        left_ref[k] = jnp.concatenate(parts, 0).T.astype(BF16)
        for c in range(2):
            u = u_k_ref[c, at].astype(F32).T
            u = jnp.concatenate([u] * 8, 1)
            u = jnp.broadcast_to(u[:, None, :], (width, 8, 8 * width)).reshape(8 * width, 8 * width)
            kron_ref[k, :, c * 8 * width : (c + 1) * 8 * width] = jnp.where(same, u, 0.0).astype(BF16)


def mode_kernel(half, modes_ref, weights_ref, mix_ref, column_ref):
    _, q_rows, modes, _ = modes_ref.shape
    first = lax.axis_index("ma") == 0
    rows = jnp.zeros((MODE_PAD - half, 2 * BRANCH_PAD), F32)
    gap = jnp.zeros((half, BRANCH_PAD - modes), F32)
    for q in range(q_rows):
        dr, di = modes_ref[0, q].astype(F32), modes_ref[1, q].astype(F32)
        parts = []
        for h in range(2):
            r, i = (jnp.where(first ^ (h == 1), d[:half], d[half:]) for d in (dr, di))
            parts += [jnp.concatenate([r, gap, i, gap], 1), rows]
            parts += [jnp.concatenate([-i, gap, r, gap], 1), rows]
        mix_ref[q] = jnp.concatenate(parts, 0).T.astype(BF16)
    w = weights_ref[...]
    w = jnp.concatenate([w, jnp.zeros((q_rows, 128 - modes), F32)], 1)
    w = jnp.concatenate([w, jnp.zeros((128 - q_rows, 128), F32)], 0).T
    for q in range(q_rows):
        column_ref[q] = w[:BRANCH_PAD, q : q + 1]


def lift(a_mat, y_refs, x_ref, first_row, width):
    quarter = MODE_PAD
    for t in range(width // 16):
        parts = []
        for u in range(2):
            lanes = slice((2 * t + u) * 8 * width, (2 * t + u + 1) * 8 * width)
            p = [ref[i * quarter : (i + 1) * quarter, lanes] for ref in y_refs for i in range(2)]
            y = jnp.concatenate(p, 0)
            turned = jnp.concatenate([-p[1], p[0], -p[3], p[2]], 0)
            rhs = jnp.concatenate(
                [jnp.concatenate([y, turned], 1), jnp.concatenate([turned, -y], 1)], 0
            )
            parts.append(lax.dot_general(a_mat, rhs, NT, preferred_element_type=F32))
        for n in range(width):
            both = jnp.concatenate([part[n * 8 : n * 8 + 8] for part in parts], 0).astype(BF16)
            for c in range(2):
                row = first_row + c * width + t * 16
                x_ref[row : row + 16, n * 128 : (n + 1) * 128] = both[:, c * 128 : (c + 1) * 128]


def lift_kernel(k, width, a_ref, *refs):
    for i in range(0, len(refs) - 1, 2):
        lift(a_ref[k], refs[i : i + 2], refs[-1], i * width, width)


def coupling_kernel(
    k, width, modes, count, early_ref, y0_ref, y1_ref, a_ref, l_ref, d_ref, w_ref, out_ref, mean_ref, late, zs
):
    q_rows = l_ref.shape[1] // width
    pitch = width + 8
    unroll = width if l_ref.shape[2] <= 512 else 4
    lift(a_ref[k], (y0_ref, y1_ref), late, 0, width)

    def columns(i):
        start = i * unroll * 128
        if not isinstance(start, int):
            start = pl.multiple_of(start, unroll * 128)
        lanes = pl.ds(start, unroll * 128)
        x = jnp.concatenate([early_ref[:, lanes], late[:, lanes]], 0)
        z = jnp.dot(l_ref[k], x, preferred_element_type=F32)
        for u in range(unroll):
            zs[pl.ds(unroll * i + u, q_rows * width, stride=pitch), :] = z[:, u * 128 : (u + 1) * 128]

    if unroll == width:
        columns(0)
    else:
        pl.loop(0, width // unroll)(columns)

    rows = width * pitch
    total = jnp.zeros((8, width * width), F32)
    for q in range(q_rows):
        z = zs[q * rows : (q + 1) * rows, :].reshape(width, pitch, 128)[:, :width]
        z = z.reshape(width * width, 128).astype(BF16)
        res = lax.dot_general(d_ref[q], z, NT, preferred_element_type=F32)
        sq = res[:BRANCH_PAD] * res[:BRANCH_PAD] + res[BRANCH_PAD:] * res[BRANCH_PAD:]
        out_ref[q] = sq[:modes].astype(BF16)
        weighted = sq * w_ref[q]
        for r in range(BRANCH_PAD // 8):
            total = total + weighted[r * 8 : r * 8 + 8]
    mean_ref[...] = jnp.sum(total, 0, keepdims=True) / count


def order_kernel(first_ref, second_ref, *refs):
    out_ref = refs[-1]
    first = lax.axis_index("ma") == 0
    for q in range(out_ref.shape[0]):
        mine, other = first_ref[q], second_ref[q]
        both = jnp.stack([jnp.where(first, mine, other), jnp.where(first, other, mine)])
        out_ref[q] = jnp.swapaxes(both, 0, 1)


def body(table, r_el, r_ph, k_coords, q_coords, u_k, u_kq, modes_q, weights_q):
    n_ea, n_pb, n_ma = lax.axis_size("ea"), lax.axis_size("pb"), lax.axis_size("ma")
    k_rows, q_rows, width = u_k.shape[1], u_kq.shape[1], u_k.shape[2]
    rows_e, half, pairs = table.shape[2], table.shape[3], table.shape[4]
    modes = n_ma * half
    shift = lambda n, s: [(i, (i + s) % n) for i in range(n)]
    flip = lambda n, s: [(i, i ^ s) for i in range(n)]

    table = jnp.transpose(table, (0, 1, 3, 2, 4))
    n_parts = n_ea * k_rows
    factor = pl.pallas_call(
        functools.partial(phase_kernel, k_rows, n_ea, rows_e, half),
        out_shape=jax.ShapeDtypeStruct((n_parts * 2 * MODE_PAD, 2 * half * rows_e), BF16),
        in_specs=[SMEM],
        out_specs=VMEM,
        cost_estimate=cost(2),
        compiler_params=pltpu.CompilerParams(vmem_limit_bytes=16 * MIB),
        name="electron_phases",
    )(jnp.concatenate([k_coords, r_el]))
    parts = pl.pallas_call(
        electron_kernel,
        out_shape=[
            jax.ShapeDtypeStruct((2 * MODE_PAD, pairs), F32 if i < k_rows else BF16)
            for i in range(n_parts)
        ],
        in_specs=[VMEM, VMEM],
        out_specs=[VMEM] * n_parts,
        cost_estimate=cost(2),
        compiler_params=pltpu.CompilerParams(vmem_limit_bytes=16 * MIB),
        name="electron_sum",
    )(factor, table)
    mine, other = [parts[0]], [lax.ppermute(parts[1], "ma", flip(n_ma, 1))]
    for s in range(1, n_ea):
        cross = [
            (e * n_ma + c, (e + s) % n_ea * n_ma + (c ^ 1)) for e in range(n_ea) for c in range(n_ma)
        ]
        mine.append(lax.ppermute(parts[s * k_rows], "ea", shift(n_ea, s)))
        other.append(lax.ppermute(parts[s * k_rows + 1], ("ea", "ma"), cross))

    masks = [0]
    distance = n_pb // 2
    while distance:
        masks += [m ^ distance for m in masks]
        distance //= 2

    left, kron = pl.pallas_call(
        functools.partial(rotation_kernel, masks),
        out_shape=[
            jax.ShapeDtypeStruct((k_rows, q_rows * width, n_pb * 2 * width), BF16),
            jax.ShapeDtypeStruct((k_rows, 8 * width, 16 * width), BF16),
        ],
        in_specs=[SMEM, SMEM, VMEM, VMEM],
        out_specs=[VMEM, VMEM],
        cost_estimate=cost(2),
        compiler_params=pltpu.CompilerParams(vmem_limit_bytes=24 * MIB),
        name="rotations",
    )(r_ph, q_coords.T, u_k, u_kq)

    mix, weights = pl.pallas_call(
        functools.partial(mode_kernel, half),
        out_shape=[
            jax.ShapeDtypeStruct((q_rows, 2 * BRANCH_PAD, n_ma * 2 * MODE_PAD), BF16),
            jax.ShapeDtypeStruct((q_rows, BRANCH_PAD, 1), F32),
        ],
        in_specs=[VMEM, VMEM],
        out_specs=[VMEM, VMEM],
        cost_estimate=cost(2),
        compiler_params=pltpu.CompilerParams(vmem_limit_bytes=16 * MIB),
        name="mode_rotation",
    )(modes_q, weights_q)

    mine[0], left, kron = lax.optimization_barrier((mine[0], left, kron))
    by_k = [sum(y.astype(F32) for y in part).astype(BF16) for part in (mine, other)]

    swap = flip(n_ma, 1)
    halves = [[y] for y in by_k]
    distance = n_pb // 2
    while distance:
        for half_blocks in halves:
            half_blocks += [lax.ppermute(y, "pb", flip(n_pb, distance)) for y in half_blocks]
        distance //= 2
    held = [y for pair in zip(*halves) for y in pair]
    swapped = [lax.ppermute(y, "ma", swap) for y in held]
    swapped = [swapped[i ^ 1] for i in range(len(swapped))]

    results = []
    for k, blocks in enumerate((held, swapped)):
        early = pl.pallas_call(
            functools.partial(lift_kernel, k, width),
            out_shape=jax.ShapeDtypeStruct(((n_pb - 1) * 2 * width, width * 128), BF16),
            in_specs=[VMEM] * (2 * n_pb - 1),
            out_specs=VMEM,
            cost_estimate=cost(1),
            compiler_params=pltpu.CompilerParams(vmem_limit_bytes=(4 + n_pb) * MIB),
            name="lift",
        )(kron, *blocks[:-2])
        results.append(
            pl.pallas_call(
                functools.partial(
                    coupling_kernel, k, width, modes, q_rows * n_pb * n_ma * modes
                ),
                out_shape=[
                    jax.ShapeDtypeStruct((q_rows, modes, pairs), BF16),
                    jax.ShapeDtypeStruct((1, pairs), F32),
                ],
                in_specs=[VMEM] * 7,
                out_specs=[VMEM, VMEM],
                scratch_shapes=[
                    pltpu.VMEM((2 * width, width * 128), BF16),
                    pltpu.VMEM((q_rows * width * (width + 8), 128), F32),
                ],
                cost_estimate=cost(4),
                compiler_params=pltpu.CompilerParams(vmem_limit_bytes=(14 + n_pb) * MIB),
                name="coupling",
            )(early, *blocks[-2:], kron, left, mix, weights)
        )
    (first, mean), (second, rest) = results
    core = lax.axis_index("ma")
    mean = jnp.where(core == 0, jnp.concatenate([mean, rest]), jnp.concatenate([rest, mean]))

    pieces = 2 if q_rows % 2 == 0 else 1
    out = None
    for i in range(pieces):
        block = (q_rows // pieces, modes, pairs)
        at = functools.partial(lambda i, j: (i, 0, 0), i)
        operands = [first, second] + ([] if out is None else [out])
        out = pl.pallas_call(
            order_kernel,
            grid=(1,),
            out_shape=jax.ShapeDtypeStruct((q_rows, modes, k_rows, pairs), BF16),
            in_specs=[pl.BlockSpec(block, at)] * 2 + [pl.BlockSpec(memory_space=pl.ANY)] * (i > 0),
            out_specs=pl.BlockSpec(
                (q_rows // pieces, modes, k_rows, pairs),
                functools.partial(lambda i, j: (i, 0, 0, 0), i),
            ),
            input_output_aliases={2: 0} if i else {},
            cost_estimate=cost(2),
            compiler_params=pltpu.CompilerParams(vmem_limit_bytes=16 * MIB),
            name="order",
        )(*operands)
    out = jnp.transpose(out, (0, 2, 1, 3))
    mean = mean + lax.ppermute(mean, "ma", swap)
    distance = 1
    while distance < n_pb:
        mean = mean + lax.ppermute(mean, "pb", flip(n_pb, distance))
        distance *= 2
    return (out, mean)


def solution(mesh):
    return jax.shard_map(
        body,
        mesh=mesh,
        in_specs=(
            P(None, "pb", "ea", "ma", None),
            P("ea", None),
            P(),
            P("grp", None),
            P(("grp", "pb"), None),
            P(None, ("grp", "ea"), None, None),
            P(None, ("grp", "pb", "ma"), "ea", None, None),
            P(None, ("grp", "pb", "ma"), None, None),
            P(("grp", "pb", "ma"), None),
        ),
        out_specs=(P(("grp", "pb", "ma"), "ea", None, None), P(("grp", "ea"), None)),
        check_vma=False,
    )
```

```python
import functools
import math

import jax
import jax.numpy as jnp
from jax import lax
from jax.experimental import pallas as pl
from jax.experimental.pallas import tpu as pltpu
from jax.sharding import PartitionSpec as P

GRID = 48
MIB = 1 << 20
NT = (((1,), (1,)), ((), ()))
F32 = jnp.float32
BF16 = jnp.bfloat16
MODE_PAD = 32
BRANCH_PAD = 64
SMEM = pl.BlockSpec(memory_space=pltpu.SMEM)
VMEM = pl.BlockSpec(memory_space=pltpu.VMEM)
HBM = pl.BlockSpec(memory_space=pltpu.HBM)


def cost(us):
    return pl.CostEstimate(flops=us * 1_000_000_000, bytes_accessed=us * 3_000_000, transcendentals=0)


def wrap(turns):
    turns = lax.rem(turns, GRID)
    return jnp.where(turns < 0, turns + GRID, turns)


def phases(turns):
    angles = turns.astype(F32) * (2.0 * math.pi / GRID)
    return jnp.cos(angles).astype(BF16).astype(F32), jnp.sin(angles).astype(BF16).astype(F32)


def phase_kernel(n_k, n_ea, rows_e, half, coords_ref, factor_ref):
    here, core = lax.axis_index("ea"), lax.axis_index("ma")
    turns = []
    for s in range(n_ea):
        for i in range(n_k):
            row = lax.rem(here + s, n_ea) * n_k + lax.rem(core + i, n_k)
            for e in range(rows_e):
                t = sum(coords_ref[row, d] * coords_ref[n_ea * n_k + e, d] for d in range(3))
                turns.append(jnp.full((1, 128), wrap(t), jnp.int32))
    cos, sin = phases(jnp.concatenate(turns, 0))
    wide = half * rows_e
    at = lax.broadcasted_iota(jnp.int32, (MODE_PAD, 2 * wide), 0)
    lane = lax.broadcasted_iota(jnp.int32, (MODE_PAD, 2 * wide), 1)
    imag = lane >= wide
    own = jnp.where(imag, lane - wide, lane) - at * rows_e
    rows = []
    for i in range(n_ea * n_k):
        for out in range(2):
            value = jnp.zeros((MODE_PAD, 2 * wide), F32)
            for e in range(rows_e):
                j = i * rows_e + e
                c, d = cos[j : j + 1, : 2 * wide], sin[j : j + 1, : 2 * wide]
                value = jnp.where(own == e, jnp.where(imag, c, d) if out else jnp.where(imag, -d, c), value)
            rows.append(value)
    factor_ref[...] = jnp.concatenate(rows, 0).astype(BF16)


def electron_kernel(factor_ref, table_ref, *outs):
    _, _, half, rows_e, pairs = table_ref.shape
    data = jnp.concatenate([table_ref[c, 0].reshape(half * rows_e, pairs) for c in range(2)], 0)
    total = jnp.dot(factor_ref[...], data, preferred_element_type=F32)
    for i, out in enumerate(outs):
        out[...] = total[i * 2 * MODE_PAD : (i + 1) * 2 * MODE_PAD].astype(out.dtype)


def rotation_kernel(masks, r_ref, q_ref, u_k_ref, u_kq_ref, left_ref, kron_ref):
    _, q_rows, n_k, width, _ = u_kq_ref.shape
    lanes = lax.broadcasted_iota(jnp.int32, (1, q_rows * width), 1) // width
    first = lax.axis_index("ma") * q_rows
    coords = []
    for d in range(3):
        line = jnp.zeros((1, q_rows * width), jnp.int32)
        for q in range(q_rows):
            line = jnp.where(lanes == q, q_ref[d, first + q], line)
        coords.append(line)
    turns = []
    for mask in masks:
        p = lax.axis_index("pb") ^ mask
        turns.append(wrap(sum(coords[d] * r_ref[p, d] for d in range(3))))
    cos, sin = phases(jnp.concatenate(turns, 0))
    row = lax.broadcasted_iota(jnp.int32, (8 * width, 8 * width), 0)
    lane = lax.broadcasted_iota(jnp.int32, (8 * width, 8 * width), 1)
    same = row % 8 == lane // width
    for k in range(n_k):
        at = lax.rem(lax.axis_index("ma") + k, n_k)
        ur, ui = (
            jnp.concatenate([u_kq_ref[c, q, at].astype(F32) for q in range(q_rows)], 1)
            for c in range(2)
        )
        parts = []
        for i in range(len(masks)):
            c, s = cos[i : i + 1], sin[i : i + 1]
            parts += [c * ur + s * ui, s * ur - c * ui]
        left_ref[k] = jnp.concatenate(parts, 0).T.astype(BF16)
        for c in range(2):
            u = u_k_ref[c, at].astype(F32).T
            u = jnp.concatenate([u] * 8, 1)
            u = jnp.broadcast_to(u[:, None, :], (width, 8, 8 * width)).reshape(8 * width, 8 * width)
            kron_ref[k, :, c * 8 * width : (c + 1) * 8 * width] = jnp.where(same, u, 0.0).astype(BF16)


def mode_kernel(half, modes_ref, weights_ref, mix_ref, column_ref):
    _, q_rows, modes, _ = modes_ref.shape
    first = lax.axis_index("ma") == 0
    rows = jnp.zeros((MODE_PAD - half, 2 * BRANCH_PAD), F32)
    gap = jnp.zeros((half, BRANCH_PAD - modes), F32)
    for q in range(q_rows):
        dr, di = modes_ref[0, q].astype(F32), modes_ref[1, q].astype(F32)
        parts = []
        for h in range(2):
            r, i = (jnp.where(first ^ (h == 1), d[:half], d[half:]) for d in (dr, di))
            parts += [jnp.concatenate([r, gap, i, gap], 1), rows]
            parts += [jnp.concatenate([-i, gap, r, gap], 1), rows]
        mix_ref[0, q] = jnp.concatenate(parts, 0).T.astype(BF16)
        mix_ref[1, q] = jnp.concatenate(parts[4:] + parts[:4], 0).T.astype(BF16)
    w = weights_ref[...]
    w = jnp.concatenate([w, jnp.zeros((q_rows, 128 - modes), F32)], 1)
    w = jnp.concatenate([w, jnp.zeros((128 - q_rows, 128), F32)], 0).T
    for q in range(q_rows):
        column_ref[q] = w[:BRANCH_PAD, q : q + 1]


def lift(a_mat, y_refs, x_ref, first_row, width):
    quarter = MODE_PAD
    for t in range(width // 16):
        parts = []
        for u in range(2):
            lanes = slice((2 * t + u) * 8 * width, (2 * t + u + 1) * 8 * width)
            p = [ref[i * quarter : (i + 1) * quarter, lanes] for ref in y_refs for i in range(2)]
            y = jnp.concatenate(p, 0)
            turned = jnp.concatenate([-p[1], p[0], -p[3], p[2]], 0)
            rhs = jnp.concatenate(
                [jnp.concatenate([y, turned], 1), jnp.concatenate([turned, -y], 1)], 0
            )
            parts.append(lax.dot_general(a_mat, rhs, NT, preferred_element_type=F32))
        for n in range(width):
            both = jnp.concatenate([part[n * 8 : n * 8 + 8] for part in parts], 0).astype(BF16)
            for c in range(2):
                row = first_row + c * width + t * 16
                x_ref[row : row + 16, n * 128 : (n + 1) * 128] = both[:, c * 128 : (c + 1) * 128]


def lift_kernel(width, a_ref, *refs):
    for i in range(0, len(refs) - 1, 2):
        lift(a_ref[0], refs[i : i + 2], refs[-1], i * width, width)


def coupling_kernel(
    k, width, modes, count, early_ref, y0_ref, y1_ref, a_ref, l_ref, d_ref, w_ref, out_ref, mean_ref, late, zs
):
    q_rows = l_ref.shape[1] // width
    pitch = width + 8
    unroll = width if l_ref.shape[2] <= 512 else 4
    lift(a_ref[k], (y0_ref, y1_ref), late, 0, width)

    def columns(i):
        start = i * unroll * 128
        if not isinstance(start, int):
            start = pl.multiple_of(start, unroll * 128)
        lanes = pl.ds(start, unroll * 128)
        x = jnp.concatenate([early_ref[:, lanes], late[:, lanes]], 0)
        z = jnp.dot(l_ref[k], x, preferred_element_type=F32)
        for u in range(unroll):
            zs[pl.ds(unroll * i + u, q_rows * width, stride=pitch), :] = z[:, u * 128 : (u + 1) * 128]

    if unroll == width:
        columns(0)
    else:
        pl.loop(0, width // unroll)(columns)

    rows = width * pitch
    total = jnp.zeros((8, width * width), F32)
    for q in range(q_rows):
        z = zs[q * rows : (q + 1) * rows, :].reshape(width, pitch, 128)[:, :width]
        z = z.reshape(width * width, 128).astype(BF16)
        res = lax.dot_general(d_ref[k, q], z, NT, preferred_element_type=F32)
        sq = res[:BRANCH_PAD] * res[:BRANCH_PAD] + res[BRANCH_PAD:] * res[BRANCH_PAD:]
        out_ref[q] = sq[:modes].astype(BF16)
        weighted = sq * w_ref[q]
        for r in range(BRANCH_PAD // 8):
            total = total + weighted[r * 8 : r * 8 + 8]
    mean_ref[...] = jnp.sum(total, 0, keepdims=True) / count


def order_kernel(first_ref, second_ref, *refs):
    out_ref = refs[-1]
    first = lax.axis_index("ma") == 0
    for q in range(out_ref.shape[0]):
        mine, other = first_ref[q], second_ref[q]
        both = jnp.stack([jnp.where(first, mine, other), jnp.where(first, other, mine)])
        out_ref[q] = jnp.swapaxes(both, 0, 1)


def body(table, r_el, r_ph, k_coords, q_coords, u_k, u_kq, modes_q, weights_q):
    n_ea, n_pb, n_ma = lax.axis_size("ea"), lax.axis_size("pb"), lax.axis_size("ma")
    k_rows, q_rows, width = u_k.shape[1], u_kq.shape[1], u_k.shape[2]
    rows_e, half, pairs = table.shape[2], table.shape[3], table.shape[4]
    modes = n_ma * half
    shift = lambda n, s: [(i, (i + s) % n) for i in range(n)]
    flip = lambda n, s: [(i, i ^ s) for i in range(n)]

    table = jnp.transpose(table, (0, 1, 3, 2, 4))
    n_parts = n_ea * k_rows
    factor = pl.pallas_call(
        functools.partial(phase_kernel, k_rows, n_ea, rows_e, half),
        out_shape=jax.ShapeDtypeStruct((n_parts * 2 * MODE_PAD, 2 * half * rows_e), BF16),
        in_specs=[SMEM],
        out_specs=VMEM,
        cost_estimate=cost(2),
        compiler_params=pltpu.CompilerParams(vmem_limit_bytes=16 * MIB),
        name="electron_phases",
    )(jnp.concatenate([k_coords, r_el]))
    parts = pl.pallas_call(
        electron_kernel,
        out_shape=[
            jax.ShapeDtypeStruct((2 * MODE_PAD, pairs), F32 if i < k_rows else BF16)
            for i in range(n_parts)
        ],
        in_specs=[VMEM, VMEM],
        out_specs=[VMEM] * n_parts,
        cost_estimate=cost(2),
        compiler_params=pltpu.CompilerParams(vmem_limit_bytes=16 * MIB),
        name="electron_sum",
    )(factor, table)
    masks = [0]
    distance = n_pb // 2
    while distance:
        masks += [m ^ distance for m in masks]
        distance //= 2

    left, kron = pl.pallas_call(
        functools.partial(rotation_kernel, masks),
        out_shape=[
            jax.ShapeDtypeStruct((k_rows, q_rows * width, n_pb * 2 * width), BF16),
            jax.ShapeDtypeStruct((k_rows, 8 * width, 16 * width), BF16),
        ],
        in_specs=[SMEM, SMEM, VMEM, VMEM],
        out_specs=[VMEM, VMEM],
        cost_estimate=cost(2),
        compiler_params=pltpu.CompilerParams(vmem_limit_bytes=24 * MIB),
        name="rotations",
    )(r_ph, q_coords.T, u_k, u_kq)

    mix, weights = pl.pallas_call(
        functools.partial(mode_kernel, half),
        out_shape=[
            jax.ShapeDtypeStruct((2, q_rows, 2 * BRANCH_PAD, n_ma * 2 * MODE_PAD), BF16),
            jax.ShapeDtypeStruct((q_rows, BRANCH_PAD, 1), F32),
        ],
        in_specs=[VMEM, VMEM],
        out_specs=[VMEM, VMEM],
        cost_estimate=cost(2),
        compiler_params=pltpu.CompilerParams(vmem_limit_bytes=16 * MIB),
        name="mode_rotation",
    )(modes_q, weights_q)

    mine, other = [parts[0]], [lax.ppermute(parts[1], "ma", flip(n_ma, 1))]
    for s in range(1, n_ea):
        cross = [
            (e * n_ma + c, (e + s) % n_ea * n_ma + (c ^ 1)) for e in range(n_ea) for c in range(n_ma)
        ]
        mine.append(lax.ppermute(parts[s * k_rows], "ea", shift(n_ea, s)))
        other.append(lax.ppermute(parts[s * k_rows + 1], ("ea", "ma"), cross))

    mine[0], left, kron = lax.optimization_barrier((mine[0], left, kron))
    by_k = [sum(y.astype(F32) for y in part).astype(BF16) for part in (mine, other)]

    swap = flip(n_ma, 1)
    halves = [[y] for y in by_k]
    distance = n_pb // 2
    while distance:
        for h, blocks in enumerate(halves):
            came = [lax.ppermute(blocks[0], "pb", flip(n_pb, distance))]
            for y in blocks[1:]:
                if h == 0:
                    y, _ = lax.optimization_barrier((y, came[0]))
                came.append(lax.ppermute(y, "pb", flip(n_pb, distance)))
            blocks += came
        distance //= 2
    held = [y for pair in zip(*halves) for y in pair]
    early = pl.pallas_call(
        functools.partial(lift_kernel, width),
        out_shape=jax.ShapeDtypeStruct(((n_pb - 1) * 2 * width, width * 128), BF16),
        in_specs=[VMEM] * (2 * n_pb - 1),
        out_specs=VMEM,
        cost_estimate=cost(1),
        compiler_params=pltpu.CompilerParams(vmem_limit_bytes=(4 + n_pb) * MIB),
        name="lift",
    )(kron, *held[:-2])
    early = (early, lax.ppermute(early, "ma", swap))
    last = (held[-2:], [lax.ppermute(y, "ma", swap) for y in held[-2:]])
    results = []
    for k in range(k_rows):
        results.append(
            pl.pallas_call(
                functools.partial(
                    coupling_kernel, k, width, modes, q_rows * n_pb * n_ma * modes
                ),
                out_shape=[
                    jax.ShapeDtypeStruct((q_rows, modes, pairs), BF16),
                    jax.ShapeDtypeStruct((1, pairs), F32),
                ],
                in_specs=[VMEM] * 7,
                out_specs=[VMEM, VMEM],
                scratch_shapes=[
                    pltpu.VMEM((2 * width, width * 128), BF16),
                    pltpu.VMEM((q_rows * width * (width + 8), 128), F32),
                ],
                cost_estimate=cost(40),
                compiler_params=pltpu.CompilerParams(vmem_limit_bytes=(14 + n_pb) * MIB),
                name="coupling",
            )(early[k], *last[k], kron, left, mix, weights)
        )
    (first, mean), (second, rest) = results
    core = lax.axis_index("ma")
    mean = jnp.where(core == 0, jnp.concatenate([mean, rest]), jnp.concatenate([rest, mean]))

    pieces = 2 if q_rows % 2 == 0 else 1
    out = None
    for i in range(pieces):
        block = (q_rows // pieces, modes, pairs)
        at = functools.partial(lambda i, j: (i, 0, 0), i)
        operands = [first, second] + ([] if out is None else [out])
        out = pl.pallas_call(
            order_kernel,
            grid=(1,),
            out_shape=jax.ShapeDtypeStruct((q_rows, modes, k_rows, pairs), BF16),
            in_specs=[pl.BlockSpec(block, at)] * 2 + [pl.BlockSpec(memory_space=pl.ANY)] * (i > 0),
            out_specs=pl.BlockSpec(
                (q_rows // pieces, modes, k_rows, pairs),
                functools.partial(lambda i, j: (i, 0, 0, 0), i),
            ),
            input_output_aliases={2: 0} if i else {},
            cost_estimate=cost(2),
            compiler_params=pltpu.CompilerParams(vmem_limit_bytes=16 * MIB),
            name="order",
        )(*operands)
    out = jnp.transpose(out, (0, 2, 1, 3))
    cross = [(z * n_ma + c, (z ^ 1) * n_ma + (c ^ 1)) for z in range(n_pb) for c in range(n_ma)]
    z_mean = lax.ppermute(mean, "pb", flip(n_pb, 1))
    c_mean = lax.ppermute(mean, ("pb", "ma"), cross)
    m_mean = lax.ppermute(mean, "ma", swap)
    mean = (mean + m_mean) + (z_mean + c_mean)
    distance = 2
    while distance < n_pb:
        mean = mean + lax.ppermute(mean, "pb", flip(n_pb, distance))
        distance *= 2
    return (out, mean)


def solution(mesh):
    return jax.shard_map(
        body,
        mesh=mesh,
        in_specs=(
            P(None, "pb", "ea", "ma", None),
            P("ea", None),
            P(),
            P("grp", None),
            P(("grp", "pb"), None),
            P(None, ("grp", "ea"), None, None),
            P(None, ("grp", "pb", "ma"), "ea", None, None),
            P(None, ("grp", "pb", "ma"), None, None),
            P(("grp", "pb", "ma"), None),
        ),
        out_specs=(P(("grp", "pb", "ma"), "ea", None, None), P(("grp", "ea"), None)),
        check_vma=False,
    )
```

```python
import functools
import math

import jax
import jax.numpy as jnp
from jax import lax
from jax.experimental import pallas as pl
from jax.experimental.pallas import tpu as pltpu
from jax.sharding import PartitionSpec as P

GRID = 48
MIB = 1 << 20
NT = (((1,), (1,)), ((), ()))
F32 = jnp.float32
BF16 = jnp.bfloat16
MODE_PAD = 32
BRANCH_PAD = 64
SMEM = pl.BlockSpec(memory_space=pltpu.SMEM)
VMEM = pl.BlockSpec(memory_space=pltpu.VMEM)
HBM = pl.BlockSpec(memory_space=pltpu.HBM)


def cost(us):
    return pl.CostEstimate(flops=us * 1_000_000_000, bytes_accessed=us * 3_000_000, transcendentals=0)


def wrap(turns):
    turns = lax.rem(turns, GRID)
    return jnp.where(turns < 0, turns + GRID, turns)


def phases(turns):
    angles = turns.astype(F32) * (2.0 * math.pi / GRID)
    return jnp.cos(angles).astype(BF16).astype(F32), jnp.sin(angles).astype(BF16).astype(F32)


def phase_kernel(n_k, n_ea, rows_e, half, coords_ref, factor_ref):
    here, core = lax.axis_index("ea"), lax.axis_index("ma")
    turns = []
    for s in range(n_ea):
        for i in range(n_k):
            row = lax.rem(here + s, n_ea) * n_k + lax.rem(core + i, n_k)
            for e in range(rows_e):
                t = sum(coords_ref[row, d] * coords_ref[n_ea * n_k + e, d] for d in range(3))
                turns.append(jnp.full((1, 128), wrap(t), jnp.int32))
    cos, sin = phases(jnp.concatenate(turns, 0))
    wide = half * rows_e
    at = lax.broadcasted_iota(jnp.int32, (2 * MODE_PAD, 2 * wide), 0)
    lane = lax.broadcasted_iota(jnp.int32, (2 * MODE_PAD, 2 * wide), 1)
    imag, to_imag = lane >= wide, at >= half
    own = jnp.where(imag, lane - wide, lane) - jnp.where(to_imag, at - half, at) * rows_e
    same = imag == to_imag
    sign = jnp.where(to_imag, 1.0, -1.0)
    for i in range(n_ea * n_k):
        value = jnp.zeros((2 * MODE_PAD, 2 * wide), F32)
        for e in range(rows_e):
            j = i * rows_e + e
            c, d = cos[j : j + 1, : 2 * wide], sin[j : j + 1, : 2 * wide]
            value = jnp.where(own == e, jnp.where(same, c, sign * d), value)
        factor_ref[i * 2 * MODE_PAD : (i + 1) * 2 * MODE_PAD] = value.astype(BF16)


def electron_kernel(factor_ref, table_ref, *outs):
    _, _, half, rows_e, pairs = table_ref.shape
    data = jnp.concatenate([table_ref[c, 0].reshape(half * rows_e, pairs) for c in range(2)], 0)
    total = jnp.dot(factor_ref[...], data, preferred_element_type=F32)
    for i, out in enumerate(outs):
        part = total[i * 2 * MODE_PAD : i * 2 * MODE_PAD + 2 * half]
        part = jnp.concatenate([part[:, : pairs // 2], part[:, pairs // 2 :]], 0)
        out[...] = part.astype(out.dtype)


def rotation_kernel(masks, r_ref, q_ref, u_k_ref, u_kq_ref, left_ref, kron_ref):
    _, q_rows, n_k, width, _ = u_kq_ref.shape
    lanes = lax.broadcasted_iota(jnp.int32, (1, q_rows * width), 1) // width
    first = lax.axis_index("ma") * q_rows
    coords = []
    for d in range(3):
        line = jnp.zeros((1, q_rows * width), jnp.int32)
        for q in range(q_rows):
            line = jnp.where(lanes == q, q_ref[d, first + q], line)
        coords.append(line)
    turns = []
    for mask in masks:
        p = lax.axis_index("pb") ^ mask
        turns.append(wrap(sum(coords[d] * r_ref[p, d] for d in range(3))))
    cos, sin = phases(jnp.concatenate(turns, 0))
    row = lax.broadcasted_iota(jnp.int32, (8 * width, 8 * width), 0)
    lane = lax.broadcasted_iota(jnp.int32, (8 * width, 8 * width), 1)
    same = row % 8 == lane // width
    for k in range(n_k):
        at = lax.rem(lax.axis_index("ma") + k, n_k)
        ur, ui = (
            jnp.concatenate([u_kq_ref[c, q, at].astype(F32) for q in range(q_rows)], 1)
            for c in range(2)
        )
        parts = []
        for i in range(len(masks)):
            c, s = cos[i : i + 1], sin[i : i + 1]
            parts += [c * ur + s * ui, s * ur - c * ui]
        left_ref[k] = jnp.concatenate(parts, 0).T.astype(BF16)
        for c in range(2):
            u = u_k_ref[c, at].astype(F32).T
            u = jnp.concatenate([u] * 8, 1)
            u = jnp.broadcast_to(u[:, None, :], (width, 8, 8 * width)).reshape(8 * width, 8 * width)
            kron_ref[k, :, c * 8 * width : (c + 1) * 8 * width] = jnp.where(same, u, 0.0).astype(BF16)


def mode_kernel(half, modes_ref, weights_ref, mix_ref, column_ref):
    _, q_rows, modes, _ = modes_ref.shape
    first = lax.axis_index("ma") == 0
    rows = jnp.zeros((MODE_PAD - half, 2 * BRANCH_PAD), F32)
    gap = jnp.zeros((half, BRANCH_PAD - modes), F32)
    for q in range(q_rows):
        dr, di = modes_ref[0, q].astype(F32), modes_ref[1, q].astype(F32)
        parts = []
        for h in range(2):
            r, i = (jnp.where(first ^ (h == 1), d[:half], d[half:]) for d in (dr, di))
            parts += [jnp.concatenate([r, gap, i, gap], 1), rows]
            parts += [jnp.concatenate([-i, gap, r, gap], 1), rows]
        mix_ref[0, q] = jnp.concatenate(parts, 0).T.astype(BF16)
        mix_ref[1, q] = jnp.concatenate(parts[4:] + parts[:4], 0).T.astype(BF16)
    w = weights_ref[...]
    w = jnp.concatenate([w, jnp.zeros((q_rows, 128 - modes), F32)], 1)
    w = jnp.concatenate([w, jnp.zeros((128 - q_rows, 128), F32)], 0).T
    for q in range(q_rows):
        column_ref[q] = w[:BRANCH_PAD, q : q + 1]


def lift(a_mat, y_refs, x_ref, first_row, width):
    half = y_refs[0].shape[0] // 4
    gap = jnp.zeros((MODE_PAD - half, 8 * width), F32)
    for t in range(width // 16):
        parts = []
        for u in range(2):
            chunk = 2 * t + u
            lanes = chunk % (width // 16) * 8 * width
            first = chunk // (width // 16) * 2 * half
            y, turned = [], []
            for ref in y_refs:
                rows = ref[:, lanes : lanes + 8 * width].astype(F32)
                r, i = rows[first : first + half], rows[first + half : first + 2 * half]
                y += [r, gap, i, gap]
                turned += [-i, gap, r, gap]
            y, turned = (jnp.concatenate(z, 0).astype(BF16) for z in (y, turned))
            rhs = jnp.concatenate(
                [jnp.concatenate([y, turned], 1), jnp.concatenate([turned, -y], 1)], 0
            )
            parts.append(lax.dot_general(a_mat, rhs, NT, preferred_element_type=F32))
        for n in range(width):
            both = jnp.concatenate([part[n * 8 : n * 8 + 8] for part in parts], 0).astype(BF16)
            for c in range(2):
                row = first_row + c * width + t * 16
                x_ref[row : row + 16, n * 128 : (n + 1) * 128] = both[:, c * 128 : (c + 1) * 128]


def lift_kernel(width, a_ref, *refs):
    for i in range(0, len(refs) - 1, 2):
        lift(a_ref[0], refs[i : i + 2], refs[-1], i * width, width)


def coupling_kernel(
    k, width, modes, count, early_ref, y0_ref, y1_ref, a_ref, l_ref, d_ref, w_ref, out_ref, mean_ref, late, zs
):
    q_rows = l_ref.shape[1] // width
    pitch = width + 8
    unroll = width if l_ref.shape[2] <= 512 else 4
    lift(a_ref[k], (y0_ref, y1_ref), late, 0, width)

    def columns(i):
        start = i * unroll * 128
        if not isinstance(start, int):
            start = pl.multiple_of(start, unroll * 128)
        lanes = pl.ds(start, unroll * 128)
        x = jnp.concatenate([early_ref[:, lanes], late[:, lanes]], 0)
        z = jnp.dot(l_ref[k], x, preferred_element_type=F32)
        for u in range(unroll):
            zs[pl.ds(unroll * i + u, q_rows * width, stride=pitch), :] = z[:, u * 128 : (u + 1) * 128]

    if unroll == width:
        columns(0)
    else:
        pl.loop(0, width // unroll)(columns)

    rows = width * pitch
    total = jnp.zeros((8, width * width), F32)
    for q in range(q_rows):
        z = zs[q * rows : (q + 1) * rows, :].reshape(width, pitch, 128)[:, :width]
        z = z.reshape(width * width, 128).astype(BF16)
        res = lax.dot_general(d_ref[k, q], z, NT, preferred_element_type=F32)
        sq = res[:BRANCH_PAD] * res[:BRANCH_PAD] + res[BRANCH_PAD:] * res[BRANCH_PAD:]
        out_ref[q] = sq[:modes].astype(BF16)
        weighted = sq * w_ref[q]
        for r in range(BRANCH_PAD // 8):
            total = total + weighted[r * 8 : r * 8 + 8]
    mean_ref[...] = jnp.sum(total, 0, keepdims=True) / count


def order_kernel(first_ref, second_ref, *refs):
    out_ref = refs[-1]
    first = lax.axis_index("ma") == 0
    for q in range(out_ref.shape[0]):
        mine, other = first_ref[q], second_ref[q]
        both = jnp.stack([jnp.where(first, mine, other), jnp.where(first, other, mine)])
        out_ref[q] = jnp.swapaxes(both, 0, 1)


def body(table, r_el, r_ph, k_coords, q_coords, u_k, u_kq, modes_q, weights_q):
    n_ea, n_pb, n_ma = lax.axis_size("ea"), lax.axis_size("pb"), lax.axis_size("ma")
    k_rows, q_rows, width = u_k.shape[1], u_kq.shape[1], u_k.shape[2]
    rows_e, half, pairs = table.shape[2], table.shape[3], table.shape[4]
    modes = n_ma * half
    shift = lambda n, s: [(i, (i + s) % n) for i in range(n)]
    flip = lambda n, s: [(i, i ^ s) for i in range(n)]

    table = jnp.transpose(table, (0, 1, 3, 2, 4))
    n_parts = n_ea * k_rows
    factor = pl.pallas_call(
        functools.partial(phase_kernel, k_rows, n_ea, rows_e, half),
        out_shape=jax.ShapeDtypeStruct((n_parts * 2 * MODE_PAD, 2 * half * rows_e), BF16),
        in_specs=[SMEM],
        out_specs=VMEM,
        cost_estimate=cost(2),
        compiler_params=pltpu.CompilerParams(vmem_limit_bytes=16 * MIB),
        name="electron_phases",
    )(jnp.concatenate([k_coords, r_el]))
    parts = pl.pallas_call(
        electron_kernel,
        out_shape=[
            jax.ShapeDtypeStruct((4 * half, pairs // 2), F32 if i < k_rows else BF16)
            for i in range(n_parts)
        ],
        in_specs=[VMEM, VMEM],
        out_specs=[VMEM] * n_parts,
        cost_estimate=cost(2),
        compiler_params=pltpu.CompilerParams(vmem_limit_bytes=16 * MIB),
        name="electron_sum",
    )(factor, table)
    masks = [0]
    distance = n_pb // 2
    while distance:
        masks += [m ^ distance for m in masks]
        distance //= 2

    left, kron = pl.pallas_call(
        functools.partial(rotation_kernel, masks),
        out_shape=[
            jax.ShapeDtypeStruct((k_rows, q_rows * width, n_pb * 2 * width), BF16),
            jax.ShapeDtypeStruct((k_rows, 8 * width, 16 * width), BF16),
        ],
        in_specs=[SMEM, SMEM, VMEM, VMEM],
        out_specs=[VMEM, VMEM],
        cost_estimate=cost(2),
        compiler_params=pltpu.CompilerParams(vmem_limit_bytes=24 * MIB),
        name="rotations",
    )(r_ph, q_coords.T, u_k, u_kq)

    mix, weights = pl.pallas_call(
        functools.partial(mode_kernel, half),
        out_shape=[
            jax.ShapeDtypeStruct((2, q_rows, 2 * BRANCH_PAD, n_ma * 2 * MODE_PAD), BF16),
            jax.ShapeDtypeStruct((q_rows, BRANCH_PAD, 1), F32),
        ],
        in_specs=[VMEM, VMEM],
        out_specs=[VMEM, VMEM],
        cost_estimate=cost(2),
        compiler_params=pltpu.CompilerParams(vmem_limit_bytes=16 * MIB),
        name="mode_rotation",
    )(modes_q, weights_q)

    mine, other = [parts[0]], [lax.ppermute(parts[1], "ma", flip(n_ma, 1))]
    for s in range(1, n_ea):
        cross = [
            (e * n_ma + c, (e + s) % n_ea * n_ma + (c ^ 1)) for e in range(n_ea) for c in range(n_ma)
        ]
        mine.append(lax.ppermute(parts[s * k_rows], "ea", shift(n_ea, s)))
        other.append(lax.ppermute(parts[s * k_rows + 1], ("ea", "ma"), cross))

    mine[0], left, kron = lax.optimization_barrier((mine[0], left, kron))
    by_k = [sum(y.astype(F32) for y in part).astype(BF16) for part in (mine, other)]

    swap = flip(n_ma, 1)
    halves = [[y] for y in by_k]
    distance = n_pb // 2
    while distance:
        for h, blocks in enumerate(halves):
            came = [lax.ppermute(blocks[0], "pb", flip(n_pb, distance))]
            for y in blocks[1:]:
                if h == 0:
                    y, _ = lax.optimization_barrier((y, came[0]))
                came.append(lax.ppermute(y, "pb", flip(n_pb, distance)))
            blocks += came
        distance //= 2
    held = [y for pair in zip(*halves) for y in pair]
    early = pl.pallas_call(
        functools.partial(lift_kernel, width),
        out_shape=jax.ShapeDtypeStruct(((n_pb - 1) * 2 * width, width * 128), BF16),
        in_specs=[VMEM] * (2 * n_pb - 1),
        out_specs=VMEM,
        cost_estimate=cost(1),
        compiler_params=pltpu.CompilerParams(vmem_limit_bytes=(4 + n_pb) * MIB),
        name="lift",
    )(kron, *held[:-2])
    early = (early, lax.ppermute(early, "ma", swap))
    last = (held[-2:], [lax.ppermute(y, "ma", swap) for y in held[-2:]])
    results = []
    for k in range(k_rows):
        results.append(
            pl.pallas_call(
                functools.partial(
                    coupling_kernel, k, width, modes, q_rows * n_pb * n_ma * modes
                ),
                out_shape=[
                    jax.ShapeDtypeStruct((q_rows, modes, pairs), BF16),
                    jax.ShapeDtypeStruct((1, pairs), F32),
                ],
                in_specs=[VMEM] * 7,
                out_specs=[VMEM, VMEM],
                scratch_shapes=[
                    pltpu.VMEM((2 * width, width * 128), BF16),
                    pltpu.VMEM((q_rows * width * (width + 8), 128), F32),
                ],
                cost_estimate=cost(40),
                compiler_params=pltpu.CompilerParams(vmem_limit_bytes=(14 + n_pb) * MIB),
                name="coupling",
            )(early[k], *last[k], kron, left, mix, weights)
        )
    (first, mean), (second, rest) = results
    core = lax.axis_index("ma")
    mean = jnp.where(core == 0, jnp.concatenate([mean, rest]), jnp.concatenate([rest, mean]))

    pieces = 2 if q_rows % 2 == 0 else 1
    out = None
    for i in range(pieces):
        block = (q_rows // pieces, modes, pairs)
        at = functools.partial(lambda i, j: (i, 0, 0), i)
        operands = [first, second] + ([] if out is None else [out])
        out = pl.pallas_call(
            order_kernel,
            grid=(1,),
            out_shape=jax.ShapeDtypeStruct((q_rows, modes, k_rows, pairs), BF16),
            in_specs=[pl.BlockSpec(block, at)] * 2 + [pl.BlockSpec(memory_space=pl.ANY)] * (i > 0),
            out_specs=pl.BlockSpec(
                (q_rows // pieces, modes, k_rows, pairs),
                functools.partial(lambda i, j: (i, 0, 0, 0), i),
            ),
            input_output_aliases={2: 0} if i else {},
            cost_estimate=cost(2),
            compiler_params=pltpu.CompilerParams(vmem_limit_bytes=16 * MIB),
            name="order",
        )(*operands)
    out = jnp.transpose(out, (0, 2, 1, 3))
    cross = [(z * n_ma + c, (z ^ 1) * n_ma + (c ^ 1)) for z in range(n_pb) for c in range(n_ma)]
    z_mean = lax.ppermute(mean, "pb", flip(n_pb, 1))
    c_mean = lax.ppermute(mean, ("pb", "ma"), cross)
    m_mean = lax.ppermute(mean, "ma", swap)
    mean = (mean + m_mean) + (z_mean + c_mean)
    distance = 2
    while distance < n_pb:
        mean = mean + lax.ppermute(mean, "pb", flip(n_pb, distance))
        distance *= 2
    return (out, mean)


def solution(mesh):
    return jax.shard_map(
        body,
        mesh=mesh,
        in_specs=(
            P(None, "pb", "ea", "ma", None),
            P("ea", None),
            P(),
            P("grp", None),
            P(("grp", "pb"), None),
            P(None, ("grp", "ea"), None, None),
            P(None, ("grp", "pb", "ma"), "ea", None, None),
            P(None, ("grp", "pb", "ma"), None, None),
            P(("grp", "pb", "ma"), None),
        ),
        out_specs=(P(("grp", "pb", "ma"), "ea", None, None), P(("grp", "ea"), None)),
        check_vma=False,
    )
```

```python
import functools
import math

import jax
import jax.numpy as jnp
from jax import lax
from jax.experimental import pallas as pl
from jax.experimental.pallas import tpu as pltpu
from jax.sharding import PartitionSpec as P

GRID = 48
MIB = 1 << 20
NT = (((1,), (1,)), ((), ()))
F32 = jnp.float32
BF16 = jnp.bfloat16
MODE_PAD = 32
BRANCH_PAD = 64
SMEM = pl.BlockSpec(memory_space=pltpu.SMEM)
VMEM = pl.BlockSpec(memory_space=pltpu.VMEM)
HBM = pl.BlockSpec(memory_space=pltpu.HBM)


def cost(us):
    return pl.CostEstimate(flops=us * 1_000_000_000, bytes_accessed=us * 3_000_000, transcendentals=0)


def wrap(turns):
    turns = lax.rem(turns, GRID)
    return jnp.where(turns < 0, turns + GRID, turns)


def phases(turns):
    angles = turns.astype(F32) * (2.0 * math.pi / GRID)
    return jnp.cos(angles).astype(BF16).astype(F32), jnp.sin(angles).astype(BF16).astype(F32)


def phase_kernel(n_k, n_ea, rows_e, half, coords_ref, factor_ref):
    here, core = lax.axis_index("ea"), lax.axis_index("ma")
    turns = []
    for s in range(n_ea):
        for i in range(n_k):
            row = lax.rem(here + s, n_ea) * n_k + lax.rem(core + i, n_k)
            for e in range(rows_e):
                t = sum(coords_ref[row, d] * coords_ref[n_ea * n_k + e, d] for d in range(3))
                turns.append(jnp.full((1, 128), wrap(t), jnp.int32))
    cos, sin = phases(jnp.concatenate(turns, 0))
    wide = half * rows_e
    at = lax.broadcasted_iota(jnp.int32, (2 * MODE_PAD, 2 * wide), 0)
    lane = lax.broadcasted_iota(jnp.int32, (2 * MODE_PAD, 2 * wide), 1)
    imag, to_imag = lane >= wide, at >= half
    own = jnp.where(imag, lane - wide, lane) - jnp.where(to_imag, at - half, at) * rows_e
    same = imag == to_imag
    sign = jnp.where(to_imag, 1.0, -1.0)
    for i in range(n_ea * n_k):
        value = jnp.zeros((2 * MODE_PAD, 2 * wide), F32)
        for e in range(rows_e):
            j = i * rows_e + e
            c, d = cos[j : j + 1, : 2 * wide], sin[j : j + 1, : 2 * wide]
            value = jnp.where(own == e, jnp.where(same, c, sign * d), value)
        factor_ref[i * 2 * MODE_PAD : (i + 1) * 2 * MODE_PAD] = value.astype(BF16)


def electron_kernel(factor_ref, table_ref, *outs):
    _, _, half, rows_e, pairs = table_ref.shape
    data = jnp.concatenate([table_ref[c, 0].reshape(half * rows_e, pairs) for c in range(2)], 0)
    total = jnp.dot(factor_ref[...], data, preferred_element_type=F32)
    for i, out in enumerate(outs):
        part = total[i * 2 * MODE_PAD : i * 2 * MODE_PAD + 2 * half]
        part = jnp.concatenate([part[:, : pairs // 2], part[:, pairs // 2 :]], 0)
        out[...] = part.astype(out.dtype)


def rotation_kernel(masks, r_ref, q_ref, u_k_ref, u_kq_ref, left_ref, kron_ref):
    _, q_rows, n_k, width, _ = u_kq_ref.shape
    lanes = lax.broadcasted_iota(jnp.int32, (1, q_rows * width), 1) // width
    first = lax.axis_index("ma") * q_rows
    coords = []
    for d in range(3):
        line = jnp.zeros((1, q_rows * width), jnp.int32)
        for q in range(q_rows):
            line = jnp.where(lanes == q, q_ref[d, first + q], line)
        coords.append(line)
    turns = []
    for mask in masks:
        p = lax.axis_index("pb") ^ mask
        turns.append(wrap(sum(coords[d] * r_ref[p, d] for d in range(3))))
    cos, sin = phases(jnp.concatenate(turns, 0))
    row = lax.broadcasted_iota(jnp.int32, (8 * width, 8 * width), 0)
    lane = lax.broadcasted_iota(jnp.int32, (8 * width, 8 * width), 1)
    same = row % 8 == lane // width
    for k in range(n_k):
        at = lax.rem(lax.axis_index("ma") + k, n_k)
        ur, ui = (
            jnp.concatenate([u_kq_ref[c, q, at].astype(F32) for q in range(q_rows)], 1)
            for c in range(2)
        )
        parts = []
        for i in range(len(masks)):
            c, s = cos[i : i + 1], sin[i : i + 1]
            parts += [c * ur + s * ui, s * ur - c * ui]
        left_ref[k] = jnp.concatenate(parts, 0).T.astype(BF16)
        for c in range(2):
            u = u_k_ref[c, at].astype(F32).T
            u = jnp.concatenate([u] * 8, 1)
            u = jnp.broadcast_to(u[:, None, :], (width, 8, 8 * width)).reshape(8 * width, 8 * width)
            kron_ref[k, :, c * 8 * width : (c + 1) * 8 * width] = jnp.where(same, u, 0.0).astype(BF16)


def mode_kernel(half, modes_ref, weights_ref, mix_ref, column_ref):
    _, q_rows, modes, _ = modes_ref.shape
    first = lax.axis_index("ma") == 0
    rows = jnp.zeros((MODE_PAD - half, 2 * BRANCH_PAD), F32)
    gap = jnp.zeros((half, BRANCH_PAD - modes), F32)
    for q in range(q_rows):
        dr, di = modes_ref[0, q].astype(F32), modes_ref[1, q].astype(F32)
        parts = []
        for h in range(2):
            r, i = (jnp.where(first ^ (h == 1), d[:half], d[half:]) for d in (dr, di))
            parts += [jnp.concatenate([r, gap, i, gap], 1), rows]
            parts += [jnp.concatenate([-i, gap, r, gap], 1), rows]
        mix_ref[0, q] = jnp.concatenate(parts, 0).T.astype(BF16)
        mix_ref[1, q] = jnp.concatenate(parts[4:] + parts[:4], 0).T.astype(BF16)
    w = weights_ref[...]
    w = jnp.concatenate([w, jnp.zeros((q_rows, 128 - modes), F32)], 1)
    w = jnp.concatenate([w, jnp.zeros((128 - q_rows, 128), F32)], 0).T
    for q in range(q_rows):
        column_ref[q] = w[:BRANCH_PAD, q : q + 1]


def lift(a_mat, y_refs, x_ref, first_row, width):
    half = y_refs[0].shape[0] // 4
    gap = jnp.zeros((MODE_PAD - half, 8 * width), F32)
    for t in range(width // 16):
        parts = []
        for u in range(2):
            chunk = 2 * t + u
            lanes = chunk % (width // 16) * 8 * width
            first = chunk // (width // 16) * 2 * half
            y, turned = [], []
            for ref in y_refs:
                rows = ref[:, lanes : lanes + 8 * width].astype(F32)
                r, i = rows[first : first + half], rows[first + half : first + 2 * half]
                y += [r, gap, i, gap]
                turned += [-i, gap, r, gap]
            y, turned = (jnp.concatenate(z, 0).astype(BF16) for z in (y, turned))
            rhs = jnp.concatenate(
                [jnp.concatenate([y, turned], 1), jnp.concatenate([turned, -y], 1)], 0
            )
            parts.append(lax.dot_general(a_mat, rhs, NT, preferred_element_type=F32))
        for n in range(width):
            both = jnp.concatenate([part[n * 8 : n * 8 + 8] for part in parts], 0).astype(BF16)
            for c in range(2):
                row = first_row + c * width + t * 16
                x_ref[row : row + 16, n * 128 : (n + 1) * 128] = both[:, c * 128 : (c + 1) * 128]


def lift_kernel(width, a_ref, *refs):
    for i in range(0, len(refs) - 1, 2):
        lift(a_ref[0], refs[i : i + 2], refs[-1], i * width, width)


def coupling_kernel(
    k, width, modes, count, early_ref, late_ref, l_ref, d_ref, w_ref, out_ref, mean_ref, zs
):
    q_rows = l_ref.shape[1] // width
    pitch = width + 8
    unroll = width if l_ref.shape[2] <= 512 else 4

    def columns(i):
        start = i * unroll * 128
        if not isinstance(start, int):
            start = pl.multiple_of(start, unroll * 128)
        lanes = pl.ds(start, unroll * 128)
        x = jnp.concatenate([early_ref[:, lanes], late_ref[:, lanes]], 0)
        z = jnp.dot(l_ref[k], x, preferred_element_type=F32)
        for u in range(unroll):
            zs[pl.ds(unroll * i + u, q_rows * width, stride=pitch), :] = z[:, u * 128 : (u + 1) * 128]

    if unroll == width:
        columns(0)
    else:
        pl.loop(0, width // unroll)(columns)

    rows = width * pitch
    total = jnp.zeros((8, width * width), F32)
    for q in range(q_rows):
        z = zs[q * rows : (q + 1) * rows, :].reshape(width, pitch, 128)[:, :width]
        z = z.reshape(width * width, 128).astype(BF16)
        res = lax.dot_general(d_ref[k, q], z, NT, preferred_element_type=F32)
        sq = res[:BRANCH_PAD] * res[:BRANCH_PAD] + res[BRANCH_PAD:] * res[BRANCH_PAD:]
        out_ref[q] = sq[:modes].astype(BF16)
        weighted = sq * w_ref[q]
        for r in range(BRANCH_PAD // 8):
            total = total + weighted[r * 8 : r * 8 + 8]
    mean_ref[...] = jnp.sum(total, 0, keepdims=True) / count


def order_kernel(first_ref, second_ref, *refs):
    out_ref = refs[-1]
    first = lax.axis_index("ma") == 0
    for q in range(out_ref.shape[0]):
        mine, other = first_ref[q], second_ref[q]
        both = jnp.stack([jnp.where(first, mine, other), jnp.where(first, other, mine)])
        out_ref[q] = jnp.swapaxes(both, 0, 1)


def body(table, r_el, r_ph, k_coords, q_coords, u_k, u_kq, modes_q, weights_q):
    n_ea, n_pb, n_ma = lax.axis_size("ea"), lax.axis_size("pb"), lax.axis_size("ma")
    k_rows, q_rows, width = u_k.shape[1], u_kq.shape[1], u_k.shape[2]
    rows_e, half, pairs = table.shape[2], table.shape[3], table.shape[4]
    modes = n_ma * half
    shift = lambda n, s: [(i, (i + s) % n) for i in range(n)]
    flip = lambda n, s: [(i, i ^ s) for i in range(n)]

    table = jnp.transpose(table, (0, 1, 3, 2, 4))
    n_parts = n_ea * k_rows
    factor = pl.pallas_call(
        functools.partial(phase_kernel, k_rows, n_ea, rows_e, half),
        out_shape=jax.ShapeDtypeStruct((n_parts * 2 * MODE_PAD, 2 * half * rows_e), BF16),
        in_specs=[SMEM],
        out_specs=VMEM,
        cost_estimate=cost(2),
        compiler_params=pltpu.CompilerParams(vmem_limit_bytes=16 * MIB),
        name="electron_phases",
    )(jnp.concatenate([k_coords, r_el]))
    parts = pl.pallas_call(
        electron_kernel,
        out_shape=[
            jax.ShapeDtypeStruct((4 * half, pairs // 2), F32 if i < k_rows else BF16)
            for i in range(n_parts)
        ],
        in_specs=[VMEM, VMEM],
        out_specs=[VMEM] * n_parts,
        cost_estimate=cost(2),
        compiler_params=pltpu.CompilerParams(vmem_limit_bytes=16 * MIB),
        name="electron_sum",
    )(factor, table)
    masks = [0]
    distance = n_pb // 2
    while distance:
        masks += [m ^ distance for m in masks]
        distance //= 2

    left, kron = pl.pallas_call(
        functools.partial(rotation_kernel, masks),
        out_shape=[
            jax.ShapeDtypeStruct((k_rows, q_rows * width, n_pb * 2 * width), BF16),
            jax.ShapeDtypeStruct((k_rows, 8 * width, 16 * width), BF16),
        ],
        in_specs=[SMEM, SMEM, VMEM, VMEM],
        out_specs=[VMEM, VMEM],
        cost_estimate=cost(2),
        compiler_params=pltpu.CompilerParams(vmem_limit_bytes=24 * MIB),
        name="rotations",
    )(r_ph, q_coords.T, u_k, u_kq)

    mix, weights = pl.pallas_call(
        functools.partial(mode_kernel, half),
        out_shape=[
            jax.ShapeDtypeStruct((2, q_rows, 2 * BRANCH_PAD, n_ma * 2 * MODE_PAD), BF16),
            jax.ShapeDtypeStruct((q_rows, BRANCH_PAD, 1), F32),
        ],
        in_specs=[VMEM, VMEM],
        out_specs=[VMEM, VMEM],
        cost_estimate=cost(2),
        compiler_params=pltpu.CompilerParams(vmem_limit_bytes=16 * MIB),
        name="mode_rotation",
    )(modes_q, weights_q)

    mine, other = [parts[0]], [lax.ppermute(parts[1], "ma", flip(n_ma, 1))]
    for s in range(1, n_ea):
        cross = [
            (e * n_ma + c, (e + s) % n_ea * n_ma + (c ^ 1)) for e in range(n_ea) for c in range(n_ma)
        ]
        mine.append(lax.ppermute(parts[s * k_rows], "ea", shift(n_ea, s)))
        late, _ = lax.optimization_barrier((parts[s * k_rows + 1], left))
        other.append(lax.ppermute(late, ("ea", "ma"), cross))

    mine[0], left, kron = lax.optimization_barrier((mine[0], left, kron))
    by_k = [sum(y.astype(F32) for y in part).astype(BF16) for part in (mine, other)]

    swap = flip(n_ma, 1)
    halves = [[y] for y in by_k]
    distance = n_pb // 2
    while distance:
        for h, blocks in enumerate(halves):
            came = [lax.ppermute(blocks[0], "pb", flip(n_pb, distance))]
            for y in blocks[1:]:
                if h == 0:
                    y, _ = lax.optimization_barrier((y, came[0]))
                came.append(lax.ppermute(y, "pb", flip(n_pb, distance)))
            blocks += came
        distance //= 2
    held = [y for pair in zip(*halves) for y in pair]
    lifted = []
    for blocks in (held[:-2], held[-2:]):
        lifted.append(
            pl.pallas_call(
                functools.partial(lift_kernel, width),
                out_shape=jax.ShapeDtypeStruct((len(blocks) * width, width * 128), BF16),
                in_specs=[VMEM] * (1 + len(blocks)),
                out_specs=VMEM,
                cost_estimate=cost(1),
                compiler_params=pltpu.CompilerParams(vmem_limit_bytes=(4 + n_pb) * MIB),
                name="lift",
            )(kron, *blocks)
        )
    lifted = (lifted, [lax.ppermute(x, "ma", swap) for x in lifted])
    results = []
    for k in range(k_rows):
        results.append(
            pl.pallas_call(
                functools.partial(
                    coupling_kernel, k, width, modes, q_rows * n_pb * n_ma * modes
                ),
                out_shape=[
                    jax.ShapeDtypeStruct((q_rows, modes, pairs), BF16),
                    jax.ShapeDtypeStruct((1, pairs), F32),
                ],
                in_specs=[VMEM] * 5,
                out_specs=[VMEM, VMEM],
                scratch_shapes=[
                    pltpu.VMEM((q_rows * width * (width + 8), 128), F32),
                ],
                cost_estimate=cost(40),
                compiler_params=pltpu.CompilerParams(vmem_limit_bytes=(14 + n_pb) * MIB),
                name="coupling",
            )(*lifted[k], left, mix, weights)
        )
    (first, mean), (second, rest) = results
    core = lax.axis_index("ma")
    mean = jnp.where(core == 0, jnp.concatenate([mean, rest]), jnp.concatenate([rest, mean]))

    pieces = 2 if q_rows % 2 == 0 else 1
    out = None
    for i in range(pieces):
        block = (q_rows // pieces, modes, pairs)
        at = functools.partial(lambda i, j: (i, 0, 0), i)
        operands = [first, second] + ([] if out is None else [out])
        out = pl.pallas_call(
            order_kernel,
            grid=(1,),
            out_shape=jax.ShapeDtypeStruct((q_rows, modes, k_rows, pairs), BF16),
            in_specs=[pl.BlockSpec(block, at)] * 2 + [pl.BlockSpec(memory_space=pl.ANY)] * (i > 0),
            out_specs=pl.BlockSpec(
                (q_rows // pieces, modes, k_rows, pairs),
                functools.partial(lambda i, j: (i, 0, 0, 0), i),
            ),
            input_output_aliases={2: 0} if i else {},
            cost_estimate=cost(2),
            compiler_params=pltpu.CompilerParams(vmem_limit_bytes=16 * MIB),
            name="order",
        )(*operands)
    out = jnp.transpose(out, (0, 2, 1, 3))
    cross = [(z * n_ma + c, (z ^ 1) * n_ma + (c ^ 1)) for z in range(n_pb) for c in range(n_ma)]
    z_mean = lax.ppermute(mean, "pb", flip(n_pb, 1))
    c_mean = lax.ppermute(mean, ("pb", "ma"), cross)
    m_mean = lax.ppermute(mean, "ma", swap)
    mean = (mean + m_mean) + (z_mean + c_mean)
    distance = 2
    while distance < n_pb:
        mean = mean + lax.ppermute(mean, "pb", flip(n_pb, distance))
        distance *= 2
    return (out, mean)


def solution(mesh):
    return jax.shard_map(
        body,
        mesh=mesh,
        in_specs=(
            P(None, "pb", "ea", "ma", None),
            P("ea", None),
            P(),
            P("grp", None),
            P(("grp", "pb"), None),
            P(None, ("grp", "ea"), None, None),
            P(None, ("grp", "pb", "ma"), "ea", None, None),
            P(None, ("grp", "pb", "ma"), None, None),
            P(("grp", "pb", "ma"), None),
        ),
        out_specs=(P(("grp", "pb", "ma"), "ea", None, None), P(("grp", "ea"), None)),
        check_vma=False,
    )
```

```python
import functools
import math

import jax
import jax.numpy as jnp
from jax import lax
from jax.experimental import pallas as pl
from jax.experimental.pallas import tpu as pltpu
from jax.sharding import PartitionSpec as P

GRID = 48
MIB = 1 << 20
NT = (((1,), (1,)), ((), ()))
F32 = jnp.float32
BF16 = jnp.bfloat16
MODE_PAD = 32
BRANCH_PAD = 64
SMEM = pl.BlockSpec(memory_space=pltpu.SMEM)
VMEM = pl.BlockSpec(memory_space=pltpu.VMEM)
HBM = pl.BlockSpec(memory_space=pltpu.HBM)


def cost(us):
    return pl.CostEstimate(flops=us * 1_000_000_000, bytes_accessed=us * 3_000_000, transcendentals=0)


def wrap(turns):
    turns = lax.rem(turns, GRID)
    return jnp.where(turns < 0, turns + GRID, turns)


def phases(turns):
    angles = turns.astype(F32) * (2.0 * math.pi / GRID)
    return jnp.cos(angles).astype(BF16).astype(F32), jnp.sin(angles).astype(BF16).astype(F32)


def phase_kernel(n_k, n_ea, rows_e, half, coords_ref, factor_ref):
    here, core = lax.axis_index("ea"), lax.axis_index("ma")
    turns = []
    for s in range(n_ea):
        for i in range(n_k):
            row = lax.rem(here + s, n_ea) * n_k + lax.rem(core + i, n_k)
            for e in range(rows_e):
                t = sum(coords_ref[row, d] * coords_ref[n_ea * n_k + e, d] for d in range(3))
                turns.append(jnp.full((1, 128), wrap(t), jnp.int32))
    cos, sin = phases(jnp.concatenate(turns, 0))
    wide = half * rows_e
    at = lax.broadcasted_iota(jnp.int32, (2 * MODE_PAD, 2 * wide), 0)
    lane = lax.broadcasted_iota(jnp.int32, (2 * MODE_PAD, 2 * wide), 1)
    imag, to_imag = lane >= wide, at >= half
    own = jnp.where(imag, lane - wide, lane) - jnp.where(to_imag, at - half, at) * rows_e
    same = imag == to_imag
    sign = jnp.where(to_imag, 1.0, -1.0)
    for i in range(n_ea * n_k):
        value = jnp.zeros((2 * MODE_PAD, 2 * wide), F32)
        for e in range(rows_e):
            j = i * rows_e + e
            c, d = cos[j : j + 1, : 2 * wide], sin[j : j + 1, : 2 * wide]
            value = jnp.where(own == e, jnp.where(same, c, sign * d), value)
        factor_ref[i * 2 * MODE_PAD : (i + 1) * 2 * MODE_PAD] = value.astype(BF16)


def electron_kernel(factor_ref, table_ref, *outs):
    _, _, half, rows_e, pairs = table_ref.shape
    data = jnp.concatenate([table_ref[c, 0].reshape(half * rows_e, pairs) for c in range(2)], 0)
    total = jnp.dot(factor_ref[...], data, preferred_element_type=F32)
    for i, out in enumerate(outs):
        part = total[i * 2 * MODE_PAD : i * 2 * MODE_PAD + 2 * half]
        part = jnp.concatenate([part[:, : pairs // 2], part[:, pairs // 2 :]], 0)
        out[...] = part.astype(out.dtype)


def rotation_kernel(masks, r_ref, q_ref, u_k_ref, u_kq_ref, left_ref, kron_ref):
    _, q_rows, n_k, width, _ = u_kq_ref.shape
    lanes = lax.broadcasted_iota(jnp.int32, (1, q_rows * width), 1) // width
    first = lax.axis_index("ma") * q_rows
    coords = []
    for d in range(3):
        line = jnp.zeros((1, q_rows * width), jnp.int32)
        for q in range(q_rows):
            line = jnp.where(lanes == q, q_ref[d, first + q], line)
        coords.append(line)
    turns = []
    for mask in masks:
        p = lax.axis_index("pb") ^ mask
        turns.append(wrap(sum(coords[d] * r_ref[p, d] for d in range(3))))
    cos, sin = phases(jnp.concatenate(turns, 0))
    row = lax.broadcasted_iota(jnp.int32, (8 * width, 8 * width), 0)
    lane = lax.broadcasted_iota(jnp.int32, (8 * width, 8 * width), 1)
    same = row % 8 == lane // width
    for k in range(n_k):
        at = lax.rem(lax.axis_index("ma") + k, n_k)
        ur, ui = (
            jnp.concatenate([u_kq_ref[c, q, at].astype(F32) for q in range(q_rows)], 1)
            for c in range(2)
        )
        parts = []
        for i in range(len(masks)):
            c, s = cos[i : i + 1], sin[i : i + 1]
            parts += [c * ur + s * ui, s * ur - c * ui]
        left_ref[k] = jnp.concatenate(parts, 0).T.astype(BF16)
        for c in range(2):
            u = u_k_ref[c, at].astype(F32).T
            u = jnp.concatenate([u] * 8, 1)
            u = jnp.broadcast_to(u[:, None, :], (width, 8, 8 * width)).reshape(8 * width, 8 * width)
            kron_ref[k, :, c * 8 * width : (c + 1) * 8 * width] = jnp.where(same, u, 0.0).astype(BF16)


def mode_kernel(half, modes_ref, weights_ref, mix_ref, column_ref):
    _, q_rows, modes, _ = modes_ref.shape
    first = lax.axis_index("ma") == 0
    rows = jnp.zeros((MODE_PAD - half, 2 * BRANCH_PAD), F32)
    gap = jnp.zeros((half, BRANCH_PAD - modes), F32)
    for q in range(q_rows):
        dr, di = modes_ref[0, q].astype(F32), modes_ref[1, q].astype(F32)
        parts = []
        for h in range(2):
            r, i = (jnp.where(first ^ (h == 1), d[:half], d[half:]) for d in (dr, di))
            parts += [jnp.concatenate([r, gap, i, gap], 1), rows]
            parts += [jnp.concatenate([-i, gap, r, gap], 1), rows]
        mix_ref[0, q] = jnp.concatenate(parts, 0).T.astype(BF16)
        mix_ref[1, q] = jnp.concatenate(parts[4:] + parts[:4], 0).T.astype(BF16)
    w = weights_ref[...]
    w = jnp.concatenate([w, jnp.zeros((q_rows, 128 - modes), F32)], 1)
    w = jnp.concatenate([w, jnp.zeros((128 - q_rows, 128), F32)], 0).T
    for q in range(q_rows):
        column_ref[q] = w[:BRANCH_PAD, q : q + 1]


def lift(a_mat, y_refs, x_ref, first_row, width):
    half = y_refs[0].shape[0] // 4
    gap = jnp.zeros((MODE_PAD - half, 8 * width), F32)
    for t in range(width // 16):
        parts = []
        for u in range(2):
            chunk = 2 * t + u
            lanes = chunk % (width // 16) * 8 * width
            first = chunk // (width // 16) * 2 * half
            y, turned = [], []
            for ref in y_refs:
                rows = ref[:, lanes : lanes + 8 * width].astype(F32)
                r, i = rows[first : first + half], rows[first + half : first + 2 * half]
                y += [r, gap, i, gap]
                turned += [-i, gap, r, gap]
            y, turned = (jnp.concatenate(z, 0).astype(BF16) for z in (y, turned))
            rhs = jnp.concatenate(
                [jnp.concatenate([y, turned], 1), jnp.concatenate([turned, -y], 1)], 0
            )
            parts.append(lax.dot_general(a_mat, rhs, NT, preferred_element_type=F32))
        for n in range(width):
            both = jnp.concatenate([part[n * 8 : n * 8 + 8] for part in parts], 0).astype(BF16)
            for c in range(2):
                row = first_row + c * width + t * 16
                x_ref[row : row + 16, n * 128 : (n + 1) * 128] = both[:, c * 128 : (c + 1) * 128]


def lift_kernel(width, a_ref, *refs):
    for i in range(0, len(refs) - 1, 2):
        lift(a_ref[0], refs[i : i + 2], refs[-1], i * width, width)


def coupling_kernel(
    k, width, modes, count, early_ref, late_ref, l_ref, d_ref, w_ref, out_ref, mean_ref, zs
):
    q_rows = l_ref.shape[1] // width
    pitch = width + 8
    unroll = width if l_ref.shape[2] <= 512 else 4

    def columns(i):
        start = i * unroll * 128
        if not isinstance(start, int):
            start = pl.multiple_of(start, unroll * 128)
        lanes = pl.ds(start, unroll * 128)
        x = jnp.concatenate([early_ref[:, lanes], late_ref[:, lanes]], 0)
        z = jnp.dot(l_ref[k], x, preferred_element_type=F32)
        for u in range(unroll):
            zs[pl.ds(unroll * i + u, q_rows * width, stride=pitch), :] = z[:, u * 128 : (u + 1) * 128]

    if unroll == width:
        columns(0)
    else:
        pl.loop(0, width // unroll)(columns)

    rows = width * pitch
    total = jnp.zeros((8, width * width), F32)
    for q in range(q_rows):
        z = zs[q * rows : (q + 1) * rows, :].reshape(width, pitch, 128)[:, :width]
        z = z.reshape(width * width, 128).astype(BF16)
        res = lax.dot_general(d_ref[k, q], z, NT, preferred_element_type=F32)
        sq = res[:BRANCH_PAD] * res[:BRANCH_PAD] + res[BRANCH_PAD:] * res[BRANCH_PAD:]
        out_ref[q] = sq[:modes].astype(BF16)
        weighted = sq * w_ref[q]
        for r in range(BRANCH_PAD // 8):
            total = total + weighted[r * 8 : r * 8 + 8]
    mean_ref[...] = jnp.sum(total, 0, keepdims=True) / count


def order_kernel(first_ref, second_ref, *refs):
    out_ref = refs[-1]
    first = lax.axis_index("ma") == 0
    for q in range(out_ref.shape[0]):
        mine, other = first_ref[q], second_ref[q]
        both = jnp.stack([jnp.where(first, mine, other), jnp.where(first, other, mine)])
        out_ref[q] = jnp.swapaxes(both, 0, 1)


def body(table, r_el, r_ph, k_coords, q_coords, u_k, u_kq, modes_q, weights_q):
    n_ea, n_pb, n_ma = lax.axis_size("ea"), lax.axis_size("pb"), lax.axis_size("ma")
    k_rows, q_rows, width = u_k.shape[1], u_kq.shape[1], u_k.shape[2]
    rows_e, half, pairs = table.shape[2], table.shape[3], table.shape[4]
    modes = n_ma * half
    shift = lambda n, s: [(i, (i + s) % n) for i in range(n)]
    flip = lambda n, s: [(i, i ^ s) for i in range(n)]

    table = jnp.transpose(table, (0, 1, 3, 2, 4))
    n_parts = n_ea * k_rows
    factor = pl.pallas_call(
        functools.partial(phase_kernel, k_rows, n_ea, rows_e, half),
        out_shape=jax.ShapeDtypeStruct((n_parts * 2 * MODE_PAD, 2 * half * rows_e), BF16),
        in_specs=[SMEM],
        out_specs=VMEM,
        cost_estimate=cost(2),
        compiler_params=pltpu.CompilerParams(vmem_limit_bytes=16 * MIB),
        name="electron_phases",
    )(jnp.concatenate([k_coords, r_el]))
    parts = pl.pallas_call(
        electron_kernel,
        out_shape=[
            jax.ShapeDtypeStruct((4 * half, pairs // 2), F32 if i < k_rows else BF16)
            for i in range(n_parts)
        ],
        in_specs=[VMEM, VMEM],
        out_specs=[VMEM] * n_parts,
        cost_estimate=cost(2),
        compiler_params=pltpu.CompilerParams(vmem_limit_bytes=16 * MIB),
        name="electron_sum",
    )(factor, table)
    masks = [0]
    distance = n_pb // 2
    while distance:
        masks += [m ^ distance for m in masks]
        distance //= 2

    left, kron = pl.pallas_call(
        functools.partial(rotation_kernel, masks),
        out_shape=[
            jax.ShapeDtypeStruct((k_rows, q_rows * width, n_pb * 2 * width), BF16),
            jax.ShapeDtypeStruct((k_rows, 8 * width, 16 * width), BF16),
        ],
        in_specs=[SMEM, SMEM, VMEM, VMEM],
        out_specs=[VMEM, VMEM],
        cost_estimate=cost(2),
        compiler_params=pltpu.CompilerParams(vmem_limit_bytes=24 * MIB),
        name="rotations",
    )(r_ph, q_coords.T, u_k, u_kq)

    mix, weights = pl.pallas_call(
        functools.partial(mode_kernel, half),
        out_shape=[
            jax.ShapeDtypeStruct((2, q_rows, 2 * BRANCH_PAD, n_ma * 2 * MODE_PAD), BF16),
            jax.ShapeDtypeStruct((q_rows, BRANCH_PAD, 1), F32),
        ],
        in_specs=[VMEM, VMEM],
        out_specs=[VMEM, VMEM],
        cost_estimate=cost(2),
        compiler_params=pltpu.CompilerParams(vmem_limit_bytes=16 * MIB),
        name="mode_rotation",
    )(modes_q, weights_q)

    mine, other = [parts[0]], [lax.ppermute(parts[1], "ma", flip(n_ma, 1))]
    for s in range(1, n_ea):
        cross = [
            (e * n_ma + c, (e + s) % n_ea * n_ma + (c ^ 1)) for e in range(n_ea) for c in range(n_ma)
        ]
        mine.append(lax.ppermute(parts[s * k_rows], "ea", shift(n_ea, s)))
        late, _ = lax.optimization_barrier((parts[s * k_rows + 1], left))
        other.append(lax.ppermute(late, ("ea", "ma"), cross))

    mine[0], left, kron = lax.optimization_barrier((mine[0], left, kron))
    by_k = [sum(y.astype(F32) for y in part).astype(BF16) for part in (mine, other)]

    swap = flip(n_ma, 1)
    halves = [[y] for y in by_k]
    distance = n_pb // 2
    while distance:
        for h, blocks in enumerate(halves):
            came = [lax.ppermute(blocks[0], "pb", flip(n_pb, distance))]
            for y in blocks[1:]:
                if h == 0:
                    y, _ = lax.optimization_barrier((y, came[0]))
                came.append(lax.ppermute(y, "pb", flip(n_pb, distance)))
            blocks += came
        distance //= 2
    held = [y for pair in zip(*halves) for y in pair]
    lifted = []
    for blocks in (held[:-2], held[-2:]):
        lifted.append(
            pl.pallas_call(
                functools.partial(lift_kernel, width),
                out_shape=jax.ShapeDtypeStruct((len(blocks) * width, width * 128), BF16),
                in_specs=[VMEM] * (1 + len(blocks)),
                out_specs=VMEM,
                cost_estimate=cost(1),
                compiler_params=pltpu.CompilerParams(vmem_limit_bytes=(4 + n_pb) * MIB),
                name="lift",
            )(kron, *blocks)
        )
    lifted = (lifted, [lax.ppermute(x, "ma", swap) for x in lifted])
    results = []
    for k in range(k_rows):
        results.append(
            pl.pallas_call(
                functools.partial(
                    coupling_kernel, k, width, modes, q_rows * n_pb * n_ma * modes
                ),
                out_shape=[
                    jax.ShapeDtypeStruct((q_rows, modes, pairs), BF16),
                    jax.ShapeDtypeStruct((1, pairs), F32),
                ],
                in_specs=[VMEM] * 5,
                out_specs=[VMEM, VMEM],
                scratch_shapes=[
                    pltpu.VMEM((q_rows * width * (width + 8), 128), F32),
                ],
                cost_estimate=cost(40),
                compiler_params=pltpu.CompilerParams(vmem_limit_bytes=(14 + n_pb) * MIB),
                name="coupling",
            )(*lifted[k], left, mix, weights)
        )
    (first, mean), (second, rest) = results
    core = lax.axis_index("ma")
    mean = jnp.where(core == 0, jnp.concatenate([mean, rest]), jnp.concatenate([rest, mean]))

    pieces = 3 if q_rows % 3 == 0 else 1
    ahead = max(pieces - 1, 1)
    block = (q_rows // pieces, modes, pairs)
    out = None
    for i, steps in ((0, ahead), (ahead, pieces - ahead)):
        if not steps:
            continue
        operands = [first, second] + ([] if out is None else [out])
        out = pl.pallas_call(
            order_kernel,
            grid=(steps,),
            out_shape=jax.ShapeDtypeStruct((q_rows, modes, k_rows, pairs), BF16),
            in_specs=[pl.BlockSpec(block, functools.partial(lambda i, j: (i + j, 0, 0), i))] * 2
            + [pl.BlockSpec(memory_space=pl.ANY)] * (i > 0),
            out_specs=pl.BlockSpec(
                (q_rows // pieces, modes, k_rows, pairs),
                functools.partial(lambda i, j: (i + j, 0, 0, 0), i),
            ),
            input_output_aliases={2: 0} if i else {},
            cost_estimate=cost(2),
            compiler_params=pltpu.CompilerParams(vmem_limit_bytes=16 * MIB),
            name="order",
        )(*operands)
    out = jnp.transpose(out, (0, 2, 1, 3))
    cross = [(z * n_ma + c, (z ^ 1) * n_ma + (c ^ 1)) for z in range(n_pb) for c in range(n_ma)]
    z_mean = lax.ppermute(mean, "pb", flip(n_pb, 1))
    c_mean = lax.ppermute(mean, ("pb", "ma"), cross)
    m_mean = lax.ppermute(mean, "ma", swap)
    mean = (mean + m_mean) + (z_mean + c_mean)
    distance = 2
    while distance < n_pb:
        mean = mean + lax.ppermute(mean, "pb", flip(n_pb, distance))
        distance *= 2
    return (out, mean)


def solution(mesh):
    return jax.shard_map(
        body,
        mesh=mesh,
        in_specs=(
            P(None, "pb", "ea", "ma", None),
            P("ea", None),
            P(),
            P("grp", None),
            P(("grp", "pb"), None),
            P(None, ("grp", "ea"), None, None),
            P(None, ("grp", "pb", "ma"), "ea", None, None),
            P(None, ("grp", "pb", "ma"), None, None),
            P(("grp", "pb", "ma"), None),
        ),
        out_specs=(P(("grp", "pb", "ma"), "ea", None, None), P(("grp", "ea"), None)),
        check_vma=False,
    )
```
